512 devices in a mesh: row: 16 (over z_hi, x, core), col: 32 (over z_lo, y).
Axes of the slice: x: 4, y: 4, z: 16 (z_hi: 2, z_lo: 8; z = z_hi * 8 + z_lo), core: 2. Of those that a mesh axis runs over, the one named last changes fastest.
Arguments:
- a_blocks: bfloat16 [384, 4096, 128], P('row', 'col'), may hold values from -6 to 6
- a_ids: int32 [16, 768], P('row', 'col'), may hold values from 0 to 31, as said below
- a_count: int32 [16, 32], P('row', 'col'), may hold values from 12 to 24, as said below
- b_blocks: bfloat16 [768, 4096, 128], P('row', 'col'), may hold values from -0.125 to 0.125
- b_ids: int32 [16, 1536], P('row', 'col'), may hold values from 0 to 31, as said below
- b_count: int32 [16, 64], P('row', 'col'), may hold values from 12 to 24, as said below
Outputs:
- product: bfloat16 [16384, 32768], P('row', 'col')
The draws below stay inside these ranges and needn't reach their ends.
Inputs may be any that keep to these rules, and one draw needn't show every extreme that they name: `a_ids`: within each panel the 24 slots name distinct blocks; slots from a_count on are padding. `a_count`: some panel has all 24 slots occupied. `b_ids`: within each panel the 24 slots name distinct blocks; slots from b_count on are padding. `b_count`: some panel has all 24 slots occupied.
All inputs are finite; a program needn't handle non-finite values.
Results may differ from the reference program's by a relative error of at most 0.001.
Values may be sent and summed in bfloat16 or wider, within the bound.
A program may use at most 64 MiB of HBM per device.

```python
import jax
import jax.numpy as jnp
from jax import lax

BLK = 128
BR = 8
BK = 4
BC = 8
TICKS = 4
RATIO = 2
SLOT_A = 24
SLOT_B = 24
N_ROW = 16
N_COL = 32


def panel_names(key, blocks, slots, panels):
    keys = jax.random.split(key, N_ROW * N_COL * panels)
    names = jax.vmap(lambda k: jax.random.permutation(k, blocks)[:slots])(keys)
    return names.reshape(N_ROW, N_COL * panels * slots).astype(jnp.int32)


def panel_counts(key, slots, panels):
    first, second = jax.random.split(key)
    total = N_ROW * N_COL * panels
    counts = jax.random.randint(first, (total,), slots // 2, slots + 1)
    full_tile = jax.random.randint(second, (), 0, total)
    counts = jnp.where(jnp.arange(total) == full_tile, slots, counts)
    return counts.reshape(N_ROW, N_COL * panels).astype(jnp.int32)


def draw_a_ids(key, part):
    key = jax.random.fold_in(key, 11)
    return panel_names(key, BR * BK, SLOT_A, 1)


def draw_a_count(key, part):
    key = jax.random.fold_in(key, 12)
    return panel_counts(key, SLOT_A, 1)


def draw_b_ids(key, part):
    key = jax.random.fold_in(key, 13)
    return panel_names(key, BK * BC, SLOT_B, RATIO)


def draw_b_count(key, part):
    key = jax.random.fold_in(key, 14)
    return panel_counts(key, SLOT_B, RATIO)


def levels(own_key, shape, pieces, low, largest):
    gain = 1.0
    for axis_at, parts in pieces:
        heights = jax.random.uniform(jax.random.fold_in(jax.random.fold_in(own_key, 6), axis_at), (parts,), jnp.float32, low / len(pieces), largest / len(pieces))
        gain = gain * jnp.repeat(jnp.exp(heights), shape[axis_at] // parts).reshape((-1,) + (1,) * (len(shape) - 1 - axis_at))
    return gain


def gaussian(own_key, shape, deviation, reach, cuts=(), kind=jnp.bfloat16):
    factor_of = levels(own_key, shape, cuts, -0.22, 0.18) if cuts else 1.0
    entries = jax.random.normal(own_key, shape, jnp.float32) * deviation * factor_of
    return jnp.minimum(jnp.maximum(entries, -reach), reach).astype(kind)


def setup_inputs(seed: int = 0) -> dict:
    seeds = jax.random.split(jax.random.key(seed), 7)
    return {
        "a_blocks": gaussian(seeds[0], (N_ROW * SLOT_A, N_COL * BLK, BLK), 1.0, 6.0, ((0, 16), (1, 32))),
        "a_ids": draw_a_ids(jax.random.fold_in(seeds[6], 71), 0),
        "a_count": draw_a_count(jax.random.fold_in(seeds[6], 71), 0),
        "b_blocks": gaussian(seeds[3], (N_ROW * RATIO * SLOT_B, N_COL * BLK, BLK), (TICKS * BK * BLK) ** -0.5, 0.125, ((0, 16), (1, 32))),
        "b_ids": draw_b_ids(jax.random.fold_in(seeds[6], 71), 0),
        "b_count": draw_b_count(jax.random.fold_in(seeds[6], 71), 0),
    }


def expand(blocks, ids, count, rows, cols):
    slots = blocks.shape[0]
    width = blocks.shape[1]
    live = jnp.arange(slots, dtype=jnp.int32) < count
    numbers = jnp.arange(rows * cols, dtype=jnp.int32)
    onehot = ((ids[None, :] == numbers[:, None]) & live[None, :]).astype(jnp.bfloat16)
    dense = jnp.dot(onehot, blocks.reshape(slots, width * width), preferred_element_type=jnp.float32).astype(jnp.bfloat16)
    return dense.reshape(rows, cols, width, width).transpose(0, 2, 1, 3).reshape(rows * width, cols * width)


def reference(a_blocks, a_ids, a_count, b_blocks, b_ids, b_count):
    a_store = a_blocks.reshape(N_ROW, SLOT_A, N_COL, BLK, BLK)
    b_store = b_blocks.reshape(N_ROW, RATIO, SLOT_B, N_COL, BLK, BLK)
    a_names = a_ids.reshape(N_ROW, N_COL, SLOT_A)
    b_names = b_ids.reshape(N_ROW, N_COL, RATIO, SLOT_B)
    b_filled = b_count.reshape(N_ROW, N_COL, RATIO)

    def one_tile(flat):
        row_i = (flat // N_COL).astype(jnp.int32)
        col_j = (flat % N_COL).astype(jnp.int32)
        total = jnp.zeros((BR * BLK, BC * BLK), jnp.float32)
        for tick in range(TICKS):
            col_a = (col_j + tick) % N_COL
            row_b = (row_i + tick) % N_ROW
            half = ((row_i + tick) // N_ROW) % RATIO
            left = expand(a_store[row_i, :, col_a], a_names[row_i, col_a], a_count[row_i, col_a], BR, BK)
            right = expand(b_store[row_b, half, :, col_j], b_names[row_b, col_j, half], b_filled[row_b, col_j, half], BK, BC)
            total = total + jnp.dot(left, right, preferred_element_type=jnp.float32)
        return total.astype(jnp.bfloat16)

    tiles = lax.map(one_tile, jnp.arange(N_ROW * N_COL, dtype=jnp.int32))
    tiles = tiles.reshape(N_ROW, N_COL, BR * BLK, BC * BLK)
    return tiles.transpose(0, 2, 1, 3).reshape(N_ROW * BR * BLK, N_COL * BC * BLK)
```

```python
import functools

import jax
import jax.numpy as jnp
from jax import lax
from jax.experimental import pallas as pl
from jax.experimental.pallas import tpu as pltpu
from jax.sharding import PartitionSpec as P

BR = 8
BK = 4
BC = 8
TICKS = 4
LANES = 8
MESH = pl.DeviceIdType.MESH


def exchange(
    n_row, n_col, a, b, ma, mb, ra, rb, ra_meta, rb_meta,
    lane_in, lane_mid, lane_out, sem_a, sem_b, sem_m, sem_l, send_sems,
):
    i, j = lax.axis_index("row"), lax.axis_index("col")
    n_zlo = n_col // 4
    n_z = n_row // LANES * n_zlo
    hop = n_z // 4
    zh, lane = i // LANES, i % LANES
    x, core = lane // 2, lane % 2
    zl, y = j // 4, j % 4
    z = zh * n_zlo + zl
    slots = a.shape[0]
    pieces = 4
    part = slots // pieces
    share = slots // LANES

    def along_z(steps):
        there = (z + steps + n_z) % n_z
        return ((there // n_zlo) * LANES + lane, (there % n_zlo) * 4 + y)

    barrier = pltpu.get_barrier_semaphore()
    away = hop * (1 - 2 * core)
    senders = [(zh * LANES + (lane + d) % LANES, j) for d in range(1, LANES)]
    senders += [((i + t) % n_row, j) for t in range(1, TICKS)]
    senders += [(i, (j + t) % n_col) for t in range(1, TICKS + 1)]
    senders += [(i, zl * 4 + (y + 1) % 4), (i, zl * 4 + (y + 3) % 4)]
    senders += [along_z(-away)]
    for sender in senders:
        pl.semaphore_signal(barrier, inc=1, device_id=sender, device_id_type=MESH)
    pl.semaphore_wait(barrier, len(senders))

    pending = []

    def send(src, dst, sem, device, slot=None):
        slot = len(pending) if slot is None else slot
        return pltpu.make_async_remote_copy(
            src_ref=src, dst_ref=dst, send_sem=send_sems.at[slot], recv_sem=sem,
            device_id=device, device_id_type=MESH,
        )

    def start(cond, make):
        slot = len(pending)
        pending.append((cond, functools.partial(make, slot)))
        if cond is None:
            make(slot).start()
        else:
            pl.when(cond)(lambda: make(slot).start())

    def arrived(ref, sem):
        pltpu.make_async_copy(ref, ref, sem).wait()

    def pa(slot, k):
        return ra.at[slot, pl.ds(k * part, part)]

    def pb(slot, k):
        return rb.at[slot, pl.ds(k * part, part)]

    for t in range(1, TICKS):
        start(None, lambda s, t=t: send(ma, ra_meta.at[t - 1], sem_m.at[t - 1], (i, (j - t + n_col) % n_col), s))
        start(None, lambda s, t=t: send(mb, rb_meta.at[t - 1], sem_m.at[t + 2], ((i - t + n_row) % n_row, j), s))

    base = slots * (1 - zh)

    @pl.when(lane < 3)
    def _():
        pltpu.make_async_copy(
            b.at[pl.ds(base + share * lane, share)], lane_in.at[lane], sem_l.at[0, lane]
        ).start()

    for d in range(1, LANES):
        to = (lane + d) % LANES
        start(
            lane < 3,
            lambda s, to=to: send(
                b.at[pl.ds(base + share * to, share)], lane_in.at[lane], sem_l.at[0, lane], (zh * LANES + to, j), s
            ),
        )

    up = (y + 2) // 3
    far = (i, (zl - 1 + y // 3 + n_zlo) % n_zlo * 4 + (y + up) % 4)
    far_slot = 3 - up
    for k in range(pieces):
        mine = a.at[pl.ds(k * part, part)]
        start(None, lambda s, k=k, mine=mine: send(mine, pa(far_slot, k), sem_a.at[far_slot, k], far, s))
        start(y > 0, lambda s, k=k, mine=mine: send(mine, pa(0, k), sem_a.at[0, k], (i, j - 1), s))
        own = b.at[pl.ds(k * part, part)]
        start(x > 0, lambda s, k=k, own=own: send(own, pb(1, k), sem_b.at[1, k], (i - 2, j), s))
        start(core == 1, lambda s, k=k, own=own: send(own, pb(0, k), sem_b.at[0, k], (i - 1, j), s))

    def lanes_first(p):
        arrived(lane_in.at[p], sem_l.at[0, p])
        start(None, lambda s: send(lane_in.at[p], lane_mid.at[p], sem_l.at[1, p], along_z(away), s))

    def lanes_second(p):
        arrived(lane_mid.at[p], sem_l.at[1, p])
        start(None, lambda s: send(lane_mid.at[p], lane_out.at[p], sem_l.at[2, p], along_z(away), s))

    def lanes_last(p):
        arrived(lane_out.at[p], sem_l.at[2, p])
        goal = 6 if p == 0 else 7
        slot = 2 if p == 2 else 1
        into = rb.at[slot, pl.ds(lane * share, share)]
        sem = sem_b.at[slot, lane // 2]

        @pl.when(lane == goal)
        def _():
            pltpu.make_async_copy(lane_out.at[p], into, sem).start()

        start(lane != goal, lambda s: send(lane_out.at[p], into, sem, (zh * LANES + goal, j), s))

    def near(to):
        return (i, zl * 4 + to)

    def forward_first(k):
        low = k < pieces // 2

        @pl.when(y == 0)
        def _():
            arrived(pa(3, k), sem_a.at[3, k])

        start(y == 0, lambda s: send(pa(3, k), pa(2, k), sem_a.at[2, k], near(1), s))
        start(y == 0, lambda s: send(pa(3, k), pa(0, k), sem_a.at[0, k], near(3), s))

        @pl.when((y == 1) | (y == 2))
        def _():
            arrived(pa(0, k), sem_a.at[0, k])

        start(y == 1, lambda s: send(pa(0, k), pa(1, k), sem_a.at[1, k], near(0), s))
        if not low:
            start(y == 2, lambda s: send(pa(0, k), pa(1, k), sem_a.at[1, k], near(1), s))

        @pl.when((y == 0) | (y == 2))
        def _():
            arrived(pa(2, k), sem_a.at[2, k])

        start(y == 2, lambda s: send(pa(2, k), pa(1, k), sem_a.at[1, k], near(3), s))
        if low:
            start(y == 0, lambda s: send(pa(2, k), pa(1, k), sem_a.at[1, k], near(1), s))

    def forward_second(k):
        low = k < pieces // 2

        @pl.when(y == 1)
        def _():
            arrived(pa(2, k), sem_a.at[2, k])

        @pl.when(y == 3)
        def _():
            arrived(pa(0, k), sem_a.at[0, k])

        if low:
            start(y == 1, lambda s: send(pa(2, k), pa(1, k), sem_a.at[1, k], near(2), s))
        else:
            start(y == 3, lambda s: send(pa(0, k), pa(1, k), sem_a.at[1, k], near(2), s))

    def forward_b(k, here):
        @pl.when(here)
        def _():
            arrived(pb(1, k), sem_b.at[1, k])

        start(here & (core == 0), lambda s: send(pb(1, k), pb(0, k), sem_b.at[0, k], (i + 1, j), s))
        start(here & (lane > 0), lambda s: send(pb(1, k), pb(2, k), sem_b.at[2, k], (i - 1, j), s))

    for p in range(3):
        lanes_first(p)
    for k in range(pieces):
        forward_first(k)
        forward_b(k, x < 3)
        forward_second(k)
        if k > 0:
            lanes_second(k - 1)
    for p in range(3):
        lanes_last(p)
    for k in range(pieces):
        forward_b(k, x == 3)

    for k in range(pieces):
        arrived(pa(1, k), sem_a.at[1, k])

        @pl.when(y == 0)
        def _():
            arrived(pa(0, k), sem_a.at[0, k])

        @pl.when(y == 3)
        def _():
            arrived(pa(2, k), sem_a.at[2, k])

        arrived(pb(0, k), sem_b.at[0, k])
        arrived(pb(2, k), sem_b.at[2, k])
    for t in range(TICKS - 1):
        arrived(ra_meta.at[t], sem_m.at[t])
        arrived(rb_meta.at[t], sem_m.at[t + 3])
    for cond, make in pending:
        if cond is None:
            make().wait_send()
        else:
            pl.when(cond)(lambda make=make: make().wait_send())


def gather_panels(n_row, n_col, a, b, ma, mb):
    block = a.shape[1:]
    slots = a.shape[0]
    share = slots // LANES
    hbm = pl.BlockSpec(memory_space=pl.ANY)
    return pl.pallas_call(
        functools.partial(exchange, n_row, n_col),
        out_shape=[
            jax.ShapeDtypeStruct((TICKS, slots) + block, a.dtype),
            jax.ShapeDtypeStruct((TICKS - 1, slots) + block, a.dtype),
            jax.ShapeDtypeStruct((TICKS - 1,) + ma.shape, jnp.int32),
            jax.ShapeDtypeStruct((TICKS - 1,) + mb.shape, jnp.int32),
        ],
        in_specs=[hbm] * 4,
        out_specs=[hbm] * 4,
        scratch_shapes=[pltpu.VMEM((3, share) + block, a.dtype)] * 3
        + [
            pltpu.SemaphoreType.DMA((4, 4)),
            pltpu.SemaphoreType.DMA((3, 4)),
            pltpu.SemaphoreType.DMA((6,)),
            pltpu.SemaphoreType.DMA((3, 3)),
            pltpu.SemaphoreType.DMA((96,)),
        ],
        compiler_params=pltpu.CompilerParams(collective_id=0, has_side_effects=True),
    )(a, b, ma, mb)


def fill(dense, at, blocks, place, rows, cols, along_rows):
    width = blocks.shape[-1]
    for number in range(rows * cols):
        r, c = number // cols, number % cols
        slot = place(number)
        block = blocks[jnp.maximum(slot - 1, 0)]
        block = jnp.where(slot > 0, block, jnp.zeros_like(block))
        r0, c0 = (at + r * width, c * width) if along_rows else (r * width, at + c * width)
        dense[r0 : r0 + width, c0 : c0 + width] = block


def multiply(n_row, ma, mb, ra_meta, rb_meta, row, a, b, ra, rb, out, left, right):
    width = a.shape[-1]
    depth = BK * width
    for t in range(TICKS):
        if t == 0:
            a_blocks, b_blocks = a, b
            a_place = lambda n: ma[0, n]
            b_place = lambda n: mb[0, n]
        else:
            half = (row[0] + t) // n_row
            a_blocks, b_blocks = ra.at[t - 1], rb.at[t - 1]
            a_place = lambda n, t=t: ra_meta[t - 1, 0, n]
            b_place = lambda n, t=t, half=half: rb_meta[t - 1, half, n]
        fill(left, t * depth, a_blocks, a_place, BR, BK, False)
        fill(right, t * depth, b_blocks, b_place, BK, BC, True)

    tile = 2 * width

    @pl.loop(0, BR * width // tile)
    def _(step):
        rows = pl.ds(pl.multiple_of(step * tile, tile), tile)
        out[rows, :] = jnp.dot(left[rows, :], right[...], preferred_element_type=jnp.float32).astype(out.dtype)


def places(ids, count, numbers):
    slot = jnp.arange(ids.shape[0], dtype=jnp.int32)
    hit = (ids[None, :] == jnp.arange(numbers, dtype=jnp.int32)[:, None]) & (slot < count)[None, :]
    return jnp.sum(jnp.where(hit, slot[None, :] + 1, 0), axis=1)


def shards(n_row, n_col, a_blocks, a_ids, a_count, b_blocks, b_ids, b_count):
    slots = a_blocks.shape[0]
    width = a_blocks.shape[1]
    a_at = places(a_ids[0], a_count[0, 0], BR * BK)
    b_at = jnp.stack(
        [places(b_ids[0, h * slots : (h + 1) * slots], b_count[0, h], BK * BC) for h in range(2)]
    )
    ma = jnp.zeros((8, 128), jnp.int32).at[0, : BR * BK].set(a_at)
    mb = jnp.zeros((8, 128), jnp.int32).at[:2, : BK * BC].set(b_at)
    ra, rb, ra_meta, rb_meta = gather_panels(n_row, n_col, a_blocks, b_blocks, ma, mb)
    row = lax.axis_index("row").astype(jnp.int32).reshape(1)
    smem = pl.BlockSpec(memory_space=pltpu.SMEM)
    depth = TICKS * BK * width

    def whole(count):
        return pl.BlockSpec((count, slots, width, width), lambda g: (0, 0, 0, 0))

    return pl.pallas_call(
        functools.partial(multiply, n_row),
        grid=(1,),
        out_shape=jax.ShapeDtypeStruct((BR * width, BC * width), jnp.bfloat16),
        in_specs=[smem] * 5
        + [
            pl.BlockSpec((slots, width, width), lambda g: (0, 0, 0)),
            pl.BlockSpec((slots, width, width), lambda g: (0, 0, 0)),
            whole(TICKS - 1),
            whole(TICKS - 1),
        ],
        out_specs=pl.BlockSpec((BR * width, BC * width), lambda g: (0, 0)),
        scratch_shapes=[
            pltpu.VMEM((BR * width, depth), jnp.bfloat16),
            pltpu.VMEM((depth, BC * width), jnp.bfloat16),
        ],
        compiler_params=pltpu.CompilerParams(vmem_limit_bytes=48 * 1024 * 1024),
        cost_estimate=pl.CostEstimate(
            flops=2 * BR * width * BC * width * depth, bytes_accessed=10 * 1024 * 1024, transcendentals=0
        ),
    )(ma, mb, ra_meta, rb_meta, row, a_blocks, b_blocks, ra, rb)


def solution(mesh):
    return jax.shard_map(
        functools.partial(shards, mesh.shape["row"], mesh.shape["col"]),
        mesh=mesh,
        in_specs=(
            P("row", "col", None),
            P("row", "col"),
            P("row", "col"),
            P("row", "col", None),
            P("row", "col"),
            P("row", "col"),
        ),
        out_specs=P("row", "col"),
        check_vma=False,
    )
```

```python
import functools

import jax
import jax.numpy as jnp
from jax import lax
from jax.experimental import pallas as pl
from jax.experimental.pallas import tpu as pltpu
from jax.sharding import PartitionSpec as P

BR = 8
BK = 4
BC = 8
TICKS = 4
LANES = 8
MESH = pl.DeviceIdType.MESH


def fill(dense, blocks, place, rows, cols):
    width = blocks.shape[-1]
    for number in range(rows * cols):
        r, c = number // cols, number % cols
        slot = place(number)
        block = blocks[jnp.maximum(slot - 1, 0)]
        block = jnp.where(slot > 0, block, jnp.zeros_like(block))
        dense[r * width : (r + 1) * width, c * width : (c + 1) * width] = block


def kernel(
    n_row, n_col, a, a_ids, a_count, b, b_ids, b_count, out,
    own_a, own_b, ra0, ra1, ra2, ra3, rb0, rb1, rb2, meta, ra_meta, rb_meta, lane_in, lane_mid, lane_out, left, right, total,
    ids_a, count_a, ids_b, count_b, slot_of,
    sem_a, sem_b, sem_m, sem_l, local_sems, meta_sems, send_sems,
):
    ra, rb = (ra0, ra1, ra2, ra3), (rb0, rb1, rb2)
    i, j = lax.axis_index("row"), lax.axis_index("col")
    n_zlo = n_col // 4
    n_z = n_row // LANES * n_zlo
    hop = n_z // 4
    zh, lane = i // LANES, i % LANES
    x, core = lane // 2, lane % 2
    zl, y = j // 4, j % 4
    z = zh * n_zlo + zl
    slots = a.shape[0]
    width = a.shape[-1]
    pieces = 4
    part = slots // pieces
    share = slots // LANES

    locals_ = [
        pltpu.make_async_copy(a_ids, ids_a, local_sems.at[0]),
        pltpu.make_async_copy(a_count, count_a, local_sems.at[1]),
        pltpu.make_async_copy(b_ids, ids_b, local_sems.at[2]),
        pltpu.make_async_copy(b_count, count_b, local_sems.at[3]),
        pltpu.make_async_copy(a, own_a, local_sems.at[4]),
        pltpu.make_async_copy(b.at[pl.ds(0, slots)], own_b, local_sems.at[5]),
    ]
    for copy in locals_:
        copy.start()

    def along_z(steps):
        there = (z + steps + n_z) % n_z
        return ((there // n_zlo) * LANES + lane, (there % n_zlo) * 4 + y)

    barrier = pltpu.get_barrier_semaphore()
    away = hop * (1 - 2 * core)
    senders = [(zh * LANES + (lane + d) % LANES, j) for d in range(1, LANES)]
    senders += [((i + t) % n_row, j) for t in range(1, TICKS)]
    senders += [(i, (j + t) % n_col) for t in range(1, TICKS + 1)]
    senders += [(i, zl * 4 + (y + 1) % 4), (i, zl * 4 + (y + 3) % 4)]
    senders += [along_z(-away)]
    for sender in senders:
        pl.semaphore_signal(barrier, inc=1, device_id=sender, device_id_type=MESH)
    pl.semaphore_wait(barrier, len(senders))

    pending = []

    def send(src, dst, sem, device, slot):
        return pltpu.make_async_remote_copy(
            src_ref=src, dst_ref=dst, send_sem=send_sems.at[slot], recv_sem=sem,
            device_id=device, device_id_type=MESH,
        )

    def start(cond, make):
        slot = len(pending)
        pending.append((cond, functools.partial(make, slot)))
        if cond is None:
            make(slot).start()
        else:
            pl.when(cond)(lambda: make(slot).start())

    def arrived(ref, sem):
        pltpu.make_async_copy(ref, ref, sem).wait()

    def pa(slot, k):
        return ra[slot].at[pl.ds(k * part, part)]

    def pb(slot, k):
        return rb[slot].at[pl.ds(k * part, part)]

    base = slots * (1 - zh)

    @pl.when(lane < 3)
    def _():
        pltpu.make_async_copy(
            b.at[pl.ds(base + share * lane, share)], lane_in.at[lane], sem_l.at[0, lane]
        ).start()

    for d in range(1, LANES):
        to = (lane + d) % LANES
        start(
            lane < 3,
            lambda s, to=to: send(
                b.at[pl.ds(base + share * to, share)], lane_in.at[lane], sem_l.at[0, lane], (zh * LANES + to, j), s
            ),
        )

    up = (y + 2) // 3
    far = (i, (zl - 1 + y // 3 + n_zlo) % n_zlo * 4 + (y + up) % 4)

    def start_far(k):
        mine = a.at[pl.ds(k * part, part)]
        start(y == 0, lambda s: send(mine, pa(3, k), sem_a.at[3, k], far, s))
        start(y > 0, lambda s: send(mine, pa(2, k), sem_a.at[2, k], far, s))

    for k in range(pieces):
        if k < 2:
            start_far(k)
        mine = a.at[pl.ds(k * part, part)]
        start(y > 0, lambda s, k=k, mine=mine: send(mine, pa(0, k), sem_a.at[0, k], (i, j - 1), s))
        own = b.at[pl.ds(k * part, part)]
        start(x > 0, lambda s, k=k, own=own: send(own, pb(1, k), sem_b.at[1, k], (i - 2, j), s))
        start(core == 1, lambda s, k=k, own=own: send(own, pb(0, k), sem_b.at[0, k], (i - 1, j), s))

    for copy in locals_[:4]:
        copy.wait()
    at_row = lax.broadcasted_iota(jnp.int32, meta.shape, 0)
    at_lane = lax.broadcasted_iota(jnp.int32, meta.shape, 1)
    found = jnp.zeros(meta.shape, jnp.int32)
    for s in range(slots):
        name = jnp.where(s < count_a[0, 0], ids_a[0, s], -1)
        found = jnp.where((at_row == 0) & (at_lane == name), s + 1, found)
        for h in range(2):
            name = jnp.where(s < count_b[0, h], ids_b[0, h * slots + s], -1)
            found = jnp.where((at_row == 1 + h) & (at_lane == name), s + 1, found)
    meta[...] = found
    for t in range(1, TICKS):
        start(None, lambda s, t=t: send(meta, ra_meta.at[t - 1], sem_m.at[t - 1], (i, (j - t + n_col) % n_col), s))
        start(None, lambda s, t=t: send(meta, rb_meta.at[t - 1], sem_m.at[t + 2], ((i - t + n_row) % n_row, j), s))
    mine_at = pltpu.make_async_copy(meta, slot_of.at[0], meta_sems.at[0])
    mine_at.start()
    mine_at.wait()
    for copy in locals_[4:]:
        copy.wait()

    tile = 2 * width

    def add_tick(t, a_at, b_at, half, a_panel, b_panel):
        fill(left, a_panel, lambda n: slot_of[a_at, 0, n], BR, BK)
        fill(right, b_panel, lambda n: slot_of[b_at, 1 + half, n], BK, BC)

        @pl.loop(0, BR * width // tile)
        def _(step):
            rows = pl.ds(pl.multiple_of(step * tile, tile), tile)
            product = jnp.dot(left[rows, :], right[...], preferred_element_type=jnp.float32)
            if t > 0:
                product = total[rows, :] + product
            if t < TICKS - 1:
                total[rows, :] = product
            else:
                out[rows, :] = product.astype(out.dtype)

    add_tick(0, 0, 0, 0, own_a, own_b)

    def lanes_first(p):
        arrived(lane_in.at[p], sem_l.at[0, p])
        start(None, lambda s: send(lane_in.at[p], lane_mid.at[p], sem_l.at[1, p], along_z(away), s))

    def lanes_second(p):
        arrived(lane_mid.at[p], sem_l.at[1, p])
        start(None, lambda s: send(lane_mid.at[p], lane_out.at[p], sem_l.at[2, p], along_z(away), s))

    def lanes_last(p):
        arrived(lane_out.at[p], sem_l.at[2, p])
        goal = 6 if p == 0 else 7
        slot = 2 if p == 2 else 1
        into = rb[slot].at[pl.ds(lane * share, share)]
        sem = sem_b.at[slot, lane // 2]

        @pl.when(lane == goal)
        def _():
            pltpu.make_async_copy(lane_out.at[p], into, sem).start()

        start(lane != goal, lambda s: send(lane_out.at[p], into, sem, (zh * LANES + goal, j), s))

    def near(to):
        return (i, zl * 4 + to)

    def forward_first(k):
        low = k < pieces // 2

        @pl.when(y == 0)
        def _():
            arrived(pa(3, k), sem_a.at[3, k])

        start(y == 0, lambda s: send(pa(3, k), pa(2, k), sem_a.at[2, k], near(1), s))
        start(y == 0, lambda s: send(pa(3, k), pa(0, k), sem_a.at[0, k], near(3), s))

        @pl.when((y == 1) | (y == 2))
        def _():
            arrived(pa(0, k), sem_a.at[0, k])

        start(y == 1, lambda s: send(pa(0, k), pa(1, k), sem_a.at[1, k], near(0), s))
        if not low:
            start(y == 2, lambda s: send(pa(0, k), pa(1, k), sem_a.at[1, k], near(1), s))

        @pl.when((y == 0) | (y == 2))
        def _():
            arrived(pa(2, k), sem_a.at[2, k])

        start(y == 2, lambda s: send(pa(2, k), pa(1, k), sem_a.at[1, k], near(3), s))
        if low:
            start(y == 0, lambda s: send(pa(2, k), pa(1, k), sem_a.at[1, k], near(1), s))

    def forward_second(k):
        low = k < pieces // 2

        @pl.when(y == 1)
        def _():
            arrived(pa(2, k), sem_a.at[2, k])

        @pl.when(y == 3)
        def _():
            arrived(pa(0, k), sem_a.at[0, k])

        if low:
            start(y == 1, lambda s: send(pa(2, k), pa(1, k), sem_a.at[1, k], near(2), s))
        else:
            start(y == 3, lambda s: send(pa(0, k), pa(1, k), sem_a.at[1, k], near(2), s))

    def forward_b(k, here):
        @pl.when(here)
        def _():
            arrived(pb(1, k), sem_b.at[1, k])

        start(here & (core == 0), lambda s: send(pb(1, k), pb(0, k), sem_b.at[0, k], (i + 1, j), s))
        start(here & (lane > 0), lambda s: send(pb(1, k), pb(2, k), sem_b.at[2, k], (i - 1, j), s))

    for p in range(3):
        lanes_first(p)
    for k in range(2, pieces):
        start_far(k)
    for k in range(2):
        forward_first(k)
        forward_b(k, x < 3)
    for p in range(3):
        lanes_second(p)
    for k in range(2, pieces):
        forward_first(k)
        forward_b(k, x < 3)
        forward_second(k - 2)
    lanes_last(0)
    forward_second(2)
    lanes_last(1)
    forward_second(3)
    lanes_last(2)
    for k in range(pieces):
        forward_b(k, x == 3)

    for t in range(TICKS - 1):
        arrived(ra_meta.at[t], sem_m.at[t])
        arrived(rb_meta.at[t], sem_m.at[t + 3])
    moves = [pltpu.make_async_copy(ra_meta.at[t], slot_of.at[1 + t], meta_sems.at[1 + t]) for t in range(TICKS - 1)]
    moves += [pltpu.make_async_copy(rb_meta.at[t], slot_of.at[4 + t], meta_sems.at[4 + t]) for t in range(TICKS - 1)]
    for move in moves:
        move.start()
    for move in moves:
        move.wait()
    for t in range(1, TICKS):
        for k in range(pieces):
            if t == 1:
                pl.when(y == 0)(lambda k=k: arrived(pa(0, k), sem_a.at[0, k]))
                arrived(pb(0, k), sem_b.at[0, k])
            if t == 2:
                arrived(pa(1, k), sem_a.at[1, k])
            if t == 3:
                pl.when(y == 3)(lambda k=k: arrived(pa(2, k), sem_a.at[2, k]))
                arrived(pb(2, k), sem_b.at[2, k])
        add_tick(t, t, 3 + t, (i + t) // n_row, ra[t - 1], rb[t - 1])
    for cond, make in pending:
        if cond is None:
            make().wait_send()
        else:
            pl.when(cond)(lambda make=make: make().wait_send())


def shards(n_row, n_col, a_blocks, a_ids, a_count, b_blocks, b_ids, b_count):
    slots = a_blocks.shape[0]
    width = a_blocks.shape[1]
    share = slots // LANES
    kind = a_blocks.dtype
    panel = (slots, width, width)
    hbm = pl.BlockSpec(memory_space=pl.ANY)
    dma = pltpu.SemaphoreType.DMA
    return pl.pallas_call(
        functools.partial(kernel, n_row, n_col),
        out_shape=jax.ShapeDtypeStruct((BR * width, BC * width), kind),
        in_specs=[hbm] * 6,
        out_specs=pl.BlockSpec(memory_space=pltpu.VMEM),
        scratch_shapes=[
            pltpu.VMEM(panel, kind) for _ in range(2 + TICKS + TICKS - 1)
        ]
        + [
            pltpu.VMEM((8, 128), jnp.int32),
            pltpu.VMEM((TICKS - 1, 8, 128), jnp.int32),
            pltpu.VMEM((TICKS - 1, 8, 128), jnp.int32),
        ]
        + [pltpu.VMEM((3, share, width, width), kind)] * 3
        + [
            pltpu.VMEM((BR * width, BK * width), kind),
            pltpu.VMEM((BK * width, BC * width), kind),
            pltpu.VMEM((BR * width, BC * width), jnp.float32),
            pltpu.SMEM(a_ids.shape, jnp.int32),
            pltpu.SMEM(a_count.shape, jnp.int32),
            pltpu.SMEM(b_ids.shape, jnp.int32),
            pltpu.SMEM(b_count.shape, jnp.int32),
            pltpu.SMEM((2 * TICKS - 1, 8, 128), jnp.int32),
            dma((4, 4)), dma((3, 4)), dma((6,)), dma((3, 3)), dma((6,)), dma((7,)), dma((96,)),
        ],
        compiler_params=pltpu.CompilerParams(
            collective_id=0, has_side_effects=True, vmem_limit_bytes=60 * 1024 * 1024
        ),
        cost_estimate=pl.CostEstimate(
            flops=2 * BR * width * BC * width * TICKS * BK * width, bytes_accessed=5 * 1024 * 1024, transcendentals=0
        ),
    )(a_blocks, a_ids, a_count, b_blocks, b_ids, b_count)


def solution(mesh):
    return jax.shard_map(
        functools.partial(shards, mesh.shape["row"], mesh.shape["col"]),
        mesh=mesh,
        in_specs=(
            P("row", "col", None),
            P("row", "col"),
            P("row", "col"),
            P("row", "col", None),
            P("row", "col"),
            P("row", "col"),
        ),
        out_specs=P("row", "col"),
        check_vma=False,
    )
```

```python
import functools

import jax
import jax.numpy as jnp
from jax import lax
from jax.experimental import pallas as pl
from jax.experimental.pallas import tpu as pltpu
from jax.sharding import PartitionSpec as P

BR = 8
BK = 4
BC = 8
TICKS = 4
LANES = 8
MESH = pl.DeviceIdType.MESH


def fill(dense, blocks, place, rows, cols):
    width = blocks.shape[-1]
    for number in range(rows * cols):
        r, c = number // cols, number % cols
        slot = place(number)
        block = blocks[jnp.maximum(slot - 1, 0)]
        block = jnp.where(slot > 0, block, jnp.zeros_like(block))
        dense[r * width : (r + 1) * width, c * width : (c + 1) * width] = block


def kernel(
    n_row, n_col, a, a_ids, a_count, b, b_ids, b_count, out,
    own_a, own_b, ra0, ra1, ra2, ra3, rb0, rb1, rb2, meta, ra_meta, rb_meta, lane_in, lane_out, left0, left1, left2, left3, right, total,
    ids_a, count_a, ids_b, count_b, slot_of,
    sem_a, sem_b, sem_m, sem_l, local_sems, meta_sems, send_sems,
):
    ra, rb = (ra0, ra1, ra2, ra3), (rb0, rb1, rb2)
    i, j = lax.axis_index("row"), lax.axis_index("col")
    n_zlo = n_col // 4
    n_z = n_row // LANES * n_zlo
    far_hop = n_z // 2 - 1
    zh, lane = i // LANES, i % LANES
    x, core = lane // 2, lane % 2
    zl, y = j // 4, j % 4
    z = zh * n_zlo + zl
    slots = a.shape[0]
    width = a.shape[-1]
    pieces = 4
    part = slots // pieces
    share = slots // LANES

    locals_ = [
        pltpu.make_async_copy(a_ids, ids_a, local_sems.at[0]),
        pltpu.make_async_copy(a_count, count_a, local_sems.at[1]),
        pltpu.make_async_copy(b_ids, ids_b, local_sems.at[2]),
        pltpu.make_async_copy(b_count, count_b, local_sems.at[3]),
        pltpu.make_async_copy(a, own_a, local_sems.at[4]),
        pltpu.make_async_copy(b.at[pl.ds(0, slots)], own_b, local_sems.at[5]),
    ]
    for copy in locals_:
        copy.start()

    def along_z(steps):
        there = (z + steps + n_z) % n_z
        return ((there // n_zlo) * LANES + lane, (there % n_zlo) * 4 + y)

    barrier = pltpu.get_barrier_semaphore()
    away = 1 - 2 * core
    senders = [(zh * LANES + (lane + d) % LANES, j) for d in range(1, LANES)]
    senders += [((i + t) % n_row, j) for t in range(1, TICKS)]
    senders += [(i, (j + t) % n_col) for t in range(1, TICKS + 1)]
    senders += [(i, zl * 4 + (y + 1) % 4), (i, zl * 4 + (y + 3) % 4)]
    senders += [along_z(-away * far_hop)]
    before = (z - away + n_z) % n_z
    senders += [((before // n_zlo) * LANES + d, (before % n_zlo) * 4 + y) for d in range(3)]
    for sender in senders:
        pl.semaphore_signal(barrier, inc=1, device_id=sender, device_id_type=MESH)
    pl.semaphore_wait(barrier, len(senders) - 3 + LANES * ((LANES + 2 - lane) // LANES))

    pending = []

    def send(src, dst, sem, device, slot):
        return pltpu.make_async_remote_copy(
            src_ref=src, dst_ref=dst, send_sem=send_sems.at[slot], recv_sem=sem,
            device_id=device, device_id_type=MESH,
        )

    def start(cond, make):
        slot = len(pending)
        pending.append((cond, functools.partial(make, slot)))
        if cond is None:
            make(slot).start()
        else:
            pl.when(cond)(lambda: make(slot).start())

    def arrived(ref, sem):
        pltpu.make_async_copy(ref, ref, sem).wait()

    def pa(slot, k):
        return ra[slot].at[pl.ds(k * part, part)]

    def pb(slot, k):
        return rb[slot].at[pl.ds(k * part, part)]

    base = slots * (1 - zh)

    for d in range(LANES):
        to = (z + 1 - 2 * (d % 2) + n_z) % n_z
        start(
            lane < 3,
            lambda s, d=d, to=to: send(
                b.at[pl.ds(base + share * d, share)], lane_in.at[lane], sem_l.at[0, lane],
                ((to // n_zlo) * LANES + d, (to % n_zlo) * 4 + y), s,
            ),
        )

    up = (y + 2) // 3
    far = (i, (zl - 1 + y // 3 + n_zlo) % n_zlo * 4 + (y + up) % 4)

    def start_far(k):
        mine = a.at[pl.ds(k * part, part)]
        start(y == 0, lambda s: send(mine, pa(3, k), sem_a.at[3, k], far, s))
        start(y > 0, lambda s: send(mine, pa(2, k), sem_a.at[2, k], far, s))

    for k in range(pieces):
        if k < 2:
            start_far(k)
        mine = a.at[pl.ds(k * part, part)]
        start(y > 0, lambda s, k=k, mine=mine: send(mine, pa(0, k), sem_a.at[0, k], (i, j - 1), s))
        own = b.at[pl.ds(k * part, part)]
        start(x > 0, lambda s, k=k, own=own: send(own, pb(1, k), sem_b.at[1, k], (i - 2, j), s))
        start(core == 1, lambda s, k=k, own=own: send(own, pb(0, k), sem_b.at[0, k], (i - 1, j), s))

    for copy in locals_[:4]:
        copy.wait()
    at_row = lax.broadcasted_iota(jnp.int32, meta.shape, 0)
    at_lane = lax.broadcasted_iota(jnp.int32, meta.shape, 1)
    found = jnp.zeros(meta.shape, jnp.int32)
    for s in range(slots):
        name = jnp.where(s < count_a[0, 0], ids_a[0, s], -1)
        found = jnp.where((at_row == 0) & (at_lane == name), s + 1, found)
        for h in range(2):
            name = jnp.where(s < count_b[0, h], ids_b[0, h * slots + s], -1)
            found = jnp.where((at_row == 1 + h) & (at_lane == name), s + 1, found)
    meta[...] = found
    for t in range(1, TICKS):
        start(None, lambda s, t=t: send(meta, ra_meta.at[t - 1], sem_m.at[t - 1], (i, (j - t + n_col) % n_col), s))
        start(None, lambda s, t=t: send(meta, rb_meta.at[t - 1], sem_m.at[t + 2], ((i - t + n_row) % n_row, j), s))
    mine_at = pltpu.make_async_copy(meta, slot_of.at[0], meta_sems.at[0])
    mine_at.start()
    mine_at.wait()
    for copy in locals_[4:]:
        copy.wait()

    tile = 2 * width

    lefts = (left0, left1, left2, left3)

    def expand_left(t, a_panel):
        fill(lefts[t], a_panel, lambda n: slot_of[t, 0, n], BR, BK)

    def add_tick(t, b_at, half, b_panel):
        left = lefts[t]
        fill(right, b_panel, lambda n: slot_of[b_at, 1 + half, n], BK, BC)

        @pl.loop(0, BR * width // tile)
        def _(step):
            rows = pl.ds(pl.multiple_of(step * tile, tile), tile)
            product = jnp.dot(left[rows, :], right[...], preferred_element_type=jnp.float32)
            if t > 0:
                product = total[rows, :] + product
            if t < TICKS - 1:
                total[rows, :] = product
            else:
                out[rows, :] = product.astype(out.dtype)

    expand_left(0, own_a)
    add_tick(0, 0, 0, own_b)

    def lanes_first(p):
        arrived(lane_in.at[p], sem_l.at[0, p])
        start(None, lambda s: send(lane_in.at[p], lane_out.at[p], sem_l.at[1, p], along_z(away * far_hop), s))

    def lanes_last(p):
        arrived(lane_out.at[p], sem_l.at[1, p])
        goal = 6 if p == 0 else 7
        slot = 2 if p == 2 else 1
        into = rb[slot].at[pl.ds(lane * share, share)]
        sem = sem_b.at[slot, lane // 2]

        @pl.when(lane == goal)
        def _():
            pltpu.make_async_copy(lane_out.at[p], into, sem).start()

        start(lane != goal, lambda s: send(lane_out.at[p], into, sem, (zh * LANES + goal, j), s))

    def near(to):
        return (i, zl * 4 + to)

    def forward_first(k):
        low = k < pieces // 2

        @pl.when(y == 0)
        def _():
            arrived(pa(3, k), sem_a.at[3, k])

        start(y == 0, lambda s: send(pa(3, k), pa(2, k), sem_a.at[2, k], near(1), s))
        start(y == 0, lambda s: send(pa(3, k), pa(0, k), sem_a.at[0, k], near(3), s))

        @pl.when((y == 1) | (y == 2))
        def _():
            arrived(pa(0, k), sem_a.at[0, k])

        start(y == 1, lambda s: send(pa(0, k), pa(1, k), sem_a.at[1, k], near(0), s))
        if not low:
            start(y == 2, lambda s: send(pa(0, k), pa(1, k), sem_a.at[1, k], near(1), s))

        @pl.when((y == 0) | (y == 2))
        def _():
            arrived(pa(2, k), sem_a.at[2, k])

        start(y == 2, lambda s: send(pa(2, k), pa(1, k), sem_a.at[1, k], near(3), s))
        if low:
            start(y == 0, lambda s: send(pa(2, k), pa(1, k), sem_a.at[1, k], near(1), s))

    def forward_second(k):
        low = k < pieces // 2

        @pl.when(y == 1)
        def _():
            arrived(pa(2, k), sem_a.at[2, k])

        @pl.when(y == 3)
        def _():
            arrived(pa(0, k), sem_a.at[0, k])

        if low:
            start(y == 1, lambda s: send(pa(2, k), pa(1, k), sem_a.at[1, k], near(2), s))
        else:
            start(y == 3, lambda s: send(pa(0, k), pa(1, k), sem_a.at[1, k], near(2), s))

    def forward_b(k, here):
        @pl.when(here)
        def _():
            arrived(pb(1, k), sem_b.at[1, k])

        start(here & (core == 0), lambda s: send(pb(1, k), pb(0, k), sem_b.at[0, k], (i + 1, j), s))
        start(here & (lane > 0), lambda s: send(pb(1, k), pb(2, k), sem_b.at[2, k], (i - 1, j), s))

    for p in range(3):
        lanes_first(p)
    for k in range(2, pieces):
        start_far(k)
    for k in range(pieces):
        forward_first(k)
        forward_b(k, x < 3)
        if k > 0:
            forward_second(k - 1)
    forward_second(pieces - 1)
    for p in range(3):
        lanes_last(p)

    for t in range(TICKS - 1):
        arrived(ra_meta.at[t], sem_m.at[t])
        arrived(rb_meta.at[t], sem_m.at[t + 3])
    moves = [pltpu.make_async_copy(ra_meta.at[t], slot_of.at[1 + t], meta_sems.at[1 + t]) for t in range(TICKS - 1)]
    moves += [pltpu.make_async_copy(rb_meta.at[t], slot_of.at[4 + t], meta_sems.at[4 + t]) for t in range(TICKS - 1)]
    for move in moves:
        move.start()
    for move in moves:
        move.wait()
    for k in range(pieces):
        pl.when(y == 0)(lambda k=k: arrived(pa(0, k), sem_a.at[0, k]))
        pl.when(y == 3)(lambda k=k: arrived(pa(2, k), sem_a.at[2, k]))
        arrived(pa(1, k), sem_a.at[1, k])
    for t in range(1, TICKS):
        expand_left(t, ra[t - 1])
    for k in range(pieces):
        forward_b(k, x == 3)
    for t in range(1, TICKS):
        if t != 2:
            for k in range(pieces):
                arrived(pb(t - 1, k), sem_b.at[t - 1, k])
        add_tick(t, 3 + t, (i + t) // n_row, rb[t - 1])
    for cond, make in pending:
        if cond is None:
            make().wait_send()
        else:
            pl.when(cond)(lambda make=make: make().wait_send())


def shards(n_row, n_col, a_blocks, a_ids, a_count, b_blocks, b_ids, b_count):
    slots = a_blocks.shape[0]
    width = a_blocks.shape[1]
    share = slots // LANES
    kind = a_blocks.dtype
    panel = (slots, width, width)
    hbm = pl.BlockSpec(memory_space=pl.ANY)
    dma = pltpu.SemaphoreType.DMA
    return pl.pallas_call(
        functools.partial(kernel, n_row, n_col),
        out_shape=jax.ShapeDtypeStruct((BR * width, BC * width), kind),
        in_specs=[hbm] * 6,
        out_specs=pl.BlockSpec(memory_space=pltpu.VMEM),
        scratch_shapes=[
            pltpu.VMEM(panel, kind) for _ in range(2 + TICKS + TICKS - 1)
        ]
        + [
            pltpu.VMEM((8, 128), jnp.int32),
            pltpu.VMEM((TICKS - 1, 8, 128), jnp.int32),
            pltpu.VMEM((TICKS - 1, 8, 128), jnp.int32),
        ]
        + [pltpu.VMEM((3, share, width, width), kind)] * 2
        + [pltpu.VMEM((BR * width, BK * width), kind)] * TICKS
        + [
            pltpu.VMEM((BK * width, BC * width), kind),
            pltpu.VMEM((BR * width, BC * width), jnp.float32),
            pltpu.SMEM(a_ids.shape, jnp.int32),
            pltpu.SMEM(a_count.shape, jnp.int32),
            pltpu.SMEM(b_ids.shape, jnp.int32),
            pltpu.SMEM(b_count.shape, jnp.int32),
            pltpu.SMEM((2 * TICKS - 1, 8, 128), jnp.int32),
            dma((4, 4)), dma((3, 4)), dma((6,)), dma((2, 3)), dma((6,)), dma((7,)), dma((96,)),
        ],
        compiler_params=pltpu.CompilerParams(
            collective_id=0, has_side_effects=True, vmem_limit_bytes=60 * 1024 * 1024
        ),
        cost_estimate=pl.CostEstimate(
            flops=2 * BR * width * BC * width * TICKS * BK * width, bytes_accessed=5 * 1024 * 1024, transcendentals=0
        ),
    )(a_blocks, a_ids, a_count, b_blocks, b_ids, b_count)


def solution(mesh):
    return jax.shard_map(
        functools.partial(shards, mesh.shape["row"], mesh.shape["col"]),
        mesh=mesh,
        in_specs=(
            P("row", "col", None),
            P("row", "col"),
            P("row", "col"),
            P("row", "col", None),
            P("row", "col"),
            P("row", "col"),
        ),
        out_specs=P("row", "col"),
        check_vma=False,
    )
```

```python
import functools

import jax
import jax.numpy as jnp
from jax import lax
from jax.experimental import pallas as pl
from jax.experimental.pallas import tpu as pltpu
from jax.sharding import PartitionSpec as P

BR = 8
BK = 4
BC = 8
TICKS = 4
LANES = 8
MESH = pl.DeviceIdType.MESH


def fill(dense, blocks, place, rows, cols):
    width = blocks.shape[-1]
    for number in range(rows * cols):
        r, c = number // cols, number % cols
        slot = place(number)
        block = blocks[jnp.maximum(slot - 1, 0)]
        block = jnp.where(slot > 0, block, jnp.zeros_like(block))
        dense[r * width : (r + 1) * width, c * width : (c + 1) * width] = block


def kernel(
    n_row, n_col, a, a_ids, a_count, b, b_ids, b_count, out,
    own_a, own_b, ra0, ra1, ra2, ra3, rb0, rb1, rb2, meta, ra_meta, rb_meta, lane_in, lane_mid, lane_out, left0, left1, left2, left3, right, total,
    ids_a, count_a, ids_b, count_b, slot_of,
    sem_a, sem_b, sem_m, sem_l, local_sems, meta_sems, send_sems,
):
    ra, rb = (ra0, ra1, ra2, ra3), (rb0, rb1, rb2)
    i, j = lax.axis_index("row"), lax.axis_index("col")
    n_zlo = n_col // 4
    n_z = n_row // LANES * n_zlo
    hop = n_z // 4
    zh, lane = i // LANES, i % LANES
    x, core = lane // 2, lane % 2
    zl, y = j // 4, j % 4
    z = zh * n_zlo + zl
    slots = a.shape[0]
    width = a.shape[-1]
    pieces = 4
    part = slots // pieces
    share = slots // LANES

    locals_ = [
        pltpu.make_async_copy(a_ids, ids_a, local_sems.at[0]),
        pltpu.make_async_copy(a_count, count_a, local_sems.at[1]),
        pltpu.make_async_copy(b_ids, ids_b, local_sems.at[2]),
        pltpu.make_async_copy(b_count, count_b, local_sems.at[3]),
        pltpu.make_async_copy(a, own_a, local_sems.at[4]),
        pltpu.make_async_copy(b.at[pl.ds(0, slots)], own_b, local_sems.at[5]),
    ]
    for copy in locals_:
        copy.start()

    def along_z(steps):
        there = (z + steps + n_z) % n_z
        return ((there // n_zlo) * LANES + lane, (there % n_zlo) * 4 + y)

    barrier = pltpu.get_barrier_semaphore()
    away = hop * (1 - 2 * core)
    senders = [(zh * LANES + (lane + d) % LANES, j) for d in range(1, LANES)]
    senders += [((i + t) % n_row, j) for t in range(1, TICKS)]
    senders += [(i, (j + t) % n_col) for t in range(1, TICKS + 1)]
    senders += [(i, zl * 4 + (y + 1) % 4), (i, zl * 4 + (y + 3) % 4)]
    senders += [along_z(-away)]
    for sender in senders:
        pl.semaphore_signal(barrier, inc=1, device_id=sender, device_id_type=MESH)
    for copy in locals_[:4]:
        copy.wait()
    at_row = lax.broadcasted_iota(jnp.int32, meta.shape, 0)
    at_lane = lax.broadcasted_iota(jnp.int32, meta.shape, 1)
    found = jnp.zeros(meta.shape, jnp.int32)
    for s in range(slots):
        name = jnp.where(s < count_a[0, 0], ids_a[0, s], -1)
        found = jnp.where((at_row == 0) & (at_lane == name), s + 1, found)
        for h in range(2):
            name = jnp.where(s < count_b[0, h], ids_b[0, h * slots + s], -1)
            found = jnp.where((at_row == 1 + h) & (at_lane == name), s + 1, found)
    meta[...] = found
    mine_at = pltpu.make_async_copy(meta, slot_of.at[0], meta_sems.at[0])
    mine_at.start()
    pl.semaphore_wait(barrier, len(senders))

    pending = []

    def send(src, dst, sem, device, slot):
        return pltpu.make_async_remote_copy(
            src_ref=src, dst_ref=dst, send_sem=send_sems.at[slot], recv_sem=sem,
            device_id=device, device_id_type=MESH,
        )

    def start(cond, make):
        slot = len(pending)
        pending.append((cond, functools.partial(make, slot)))
        if cond is None:
            make(slot).start()
        else:
            pl.when(cond)(lambda: make(slot).start())

    def arrived(ref, sem):
        pltpu.make_async_copy(ref, ref, sem).wait()

    def pa(slot, k):
        return ra[slot].at[pl.ds(k * part, part)]

    def pb(slot, k):
        return rb[slot].at[pl.ds(k * part, part)]

    base = slots * (1 - zh)

    @pl.when(lane < 3)
    def _():
        pltpu.make_async_copy(
            b.at[pl.ds(base + share * lane, share)], lane_in.at[lane], sem_l.at[0, lane]
        ).start()

    for d in range(1, LANES):
        to = (lane + d) % LANES
        start(
            lane < 3,
            lambda s, to=to: send(
                b.at[pl.ds(base + share * to, share)], lane_in.at[lane], sem_l.at[0, lane], (zh * LANES + to, j), s
            ),
        )

    up = (y + 2) // 3
    far = (i, (zl - 1 + y // 3 + n_zlo) % n_zlo * 4 + (y + up) % 4)

    def start_far(k):
        mine = a.at[pl.ds(k * part, part)]
        start(y == 0, lambda s: send(mine, pa(3, k), sem_a.at[3, k], far, s))
        start(y > 0, lambda s: send(mine, pa(2, k), sem_a.at[2, k], far, s))

    for k in range(pieces):
        if k < 2:
            start_far(k)
        mine = a.at[pl.ds(k * part, part)]
        start(y > 0, lambda s, k=k, mine=mine: send(mine, pa(0, k), sem_a.at[0, k], (i, j - 1), s))
        own = b.at[pl.ds(k * part, part)]
        start(x > 0, lambda s, k=k, own=own: send(own, pb(1, k), sem_b.at[1, k], (i - 2, j), s))
        start(core == 1, lambda s, k=k, own=own: send(own, pb(0, k), sem_b.at[0, k], (i - 1, j), s))

    for t in range(1, TICKS):
        start(None, lambda s, t=t: send(meta, ra_meta.at[t - 1], sem_m.at[t - 1], (i, (j - t + n_col) % n_col), s))
        start(None, lambda s, t=t: send(meta, rb_meta.at[t - 1], sem_m.at[t + 2], ((i - t + n_row) % n_row, j), s))
    mine_at.wait()
    for copy in locals_[4:]:
        copy.wait()

    tile = 2 * width

    lefts = (left0, left1, left2, left3)

    def expand_left(t, a_panel):
        fill(lefts[t], a_panel, lambda n: slot_of[t, 0, n], BR, BK)

    def add_tick(t, b_at, half, b_panel):
        left = lefts[t]
        fill(right, b_panel, lambda n: slot_of[b_at, 1 + half, n], BK, BC)

        @pl.loop(0, BR * width // tile)
        def _(step):
            rows = pl.ds(pl.multiple_of(step * tile, tile), tile)
            product = jnp.dot(left[rows, :], right[...], preferred_element_type=jnp.float32)
            if t > 0:
                product = total[rows, :] + product
            if t < TICKS - 1:
                total[rows, :] = product
            else:
                out[rows, :] = product.astype(out.dtype)

    expand_left(0, own_a)
    add_tick(0, 0, 0, own_b)

    def lanes_first(p):
        arrived(lane_in.at[p], sem_l.at[0, p])
        start(None, lambda s: send(lane_in.at[p], lane_mid.at[p], sem_l.at[1, p], along_z(away), s))

    def lanes_second(p):
        arrived(lane_mid.at[p], sem_l.at[1, p])
        start(None, lambda s: send(lane_mid.at[p], lane_out.at[p], sem_l.at[2, p], along_z(away), s))

    def lanes_last(p):
        arrived(lane_out.at[p], sem_l.at[2, p])
        for goal, slot in (((6, 1), (5, 2)), ((7, 1),), ((7, 2),))[p]:
            into = rb[slot].at[pl.ds(lane * share, share)]
            sem = sem_b.at[slot, lane // 2]

            @pl.when(lane == goal)
            def _():
                pltpu.make_async_copy(lane_out.at[p], into, sem).start()

            start(
                lane != goal,
                lambda s, goal=goal, into=into, sem=sem: send(lane_out.at[p], into, sem, (zh * LANES + goal, j), s),
            )

    def near(to):
        return (i, zl * 4 + to)

    def forward_first(k):
        low = k < pieces // 2

        @pl.when(y == 0)
        def _():
            arrived(pa(3, k), sem_a.at[3, k])

        start(y == 0, lambda s: send(pa(3, k), pa(2, k), sem_a.at[2, k], near(1), s))
        start(y == 0, lambda s: send(pa(3, k), pa(0, k), sem_a.at[0, k], near(3), s))

        @pl.when((y == 1) | (y == 2))
        def _():
            arrived(pa(0, k), sem_a.at[0, k])

        start(y == 1, lambda s: send(pa(0, k), pa(1, k), sem_a.at[1, k], near(0), s))
        if not low:
            start(y == 2, lambda s: send(pa(0, k), pa(1, k), sem_a.at[1, k], near(1), s))

        @pl.when((y == 0) | (y == 2))
        def _():
            arrived(pa(2, k), sem_a.at[2, k])

        start(y == 2, lambda s: send(pa(2, k), pa(1, k), sem_a.at[1, k], near(3), s))
        if low:
            start(y == 0, lambda s: send(pa(2, k), pa(1, k), sem_a.at[1, k], near(1), s))

    def forward_second(k):
        low = k < pieces // 2

        @pl.when(y == 1)
        def _():
            arrived(pa(2, k), sem_a.at[2, k])

        @pl.when(y == 3)
        def _():
            arrived(pa(0, k), sem_a.at[0, k])

        if low:
            start(y == 1, lambda s: send(pa(2, k), pa(1, k), sem_a.at[1, k], near(2), s))
        else:
            start(y == 3, lambda s: send(pa(0, k), pa(1, k), sem_a.at[1, k], near(2), s))

    def forward_b(k, here, back):
        @pl.when(here)
        def _():
            arrived(pb(1, k), sem_b.at[1, k])

        start(here & (core == 0), lambda s: send(pb(1, k), pb(0, k), sem_b.at[0, k], (i + 1, j), s))
        start(back, lambda s: send(pb(1, k), pb(2, k), sem_b.at[2, k], (i - 1, j), s))

    for p in range(3):
        lanes_first(p)
    for k in range(2, pieces):
        start_far(k)
    for k in range(2):
        forward_first(k)
        forward_b(k, x < 3, (x < 3) & (lane > 0))
    for p in range(3):
        lanes_second(p)
    for k in range(2, pieces):
        forward_first(k)
        forward_b(k, x < 3, (x < 3) & (lane > 0))
        forward_second(k - 2)
    forward_second(2)
    lanes_last(0)
    forward_second(3)
    lanes_last(1)
    lanes_last(2)
    for k in range(pieces):
        forward_b(k, x == 3, lane == LANES - 1)

    for t in range(TICKS - 1):
        arrived(ra_meta.at[t], sem_m.at[t])
        arrived(rb_meta.at[t], sem_m.at[t + 3])
    moves = [pltpu.make_async_copy(ra_meta.at[t], slot_of.at[1 + t], meta_sems.at[1 + t]) for t in range(TICKS - 1)]
    moves += [pltpu.make_async_copy(rb_meta.at[t], slot_of.at[4 + t], meta_sems.at[4 + t]) for t in range(TICKS - 1)]
    for move in moves:
        move.start()
    for move in moves:
        move.wait()
    for k in range(pieces):
        pl.when(y == 0)(lambda k=k: arrived(pa(0, k), sem_a.at[0, k]))
        pl.when(y == 3)(lambda k=k: arrived(pa(2, k), sem_a.at[2, k]))
        arrived(pa(1, k), sem_a.at[1, k])
    for t in range(1, TICKS):
        expand_left(t, ra[t - 1])
    for t in range(1, TICKS):
        if t != 2:
            for k in range(pieces):
                arrived(pb(t - 1, k), sem_b.at[t - 1, k])
        add_tick(t, 3 + t, (i + t) // n_row, rb[t - 1])
    for cond, make in pending:
        if cond is None:
            make().wait_send()
        else:
            pl.when(cond)(lambda make=make: make().wait_send())


def shards(n_row, n_col, a_blocks, a_ids, a_count, b_blocks, b_ids, b_count):
    slots = a_blocks.shape[0]
    width = a_blocks.shape[1]
    share = slots // LANES
    kind = a_blocks.dtype
    panel = (slots, width, width)
    hbm = pl.BlockSpec(memory_space=pl.ANY)
    dma = pltpu.SemaphoreType.DMA
    return pl.pallas_call(
        functools.partial(kernel, n_row, n_col),
        out_shape=jax.ShapeDtypeStruct((BR * width, BC * width), kind),
        in_specs=[hbm] * 6,
        out_specs=pl.BlockSpec(memory_space=pltpu.VMEM),
        scratch_shapes=[
            pltpu.VMEM(panel, kind) for _ in range(2 + TICKS + TICKS - 1)
        ]
        + [
            pltpu.VMEM((8, 128), jnp.int32),
            pltpu.VMEM((TICKS - 1, 8, 128), jnp.int32),
            pltpu.VMEM((TICKS - 1, 8, 128), jnp.int32),
        ]
        + [pltpu.VMEM((3, share, width, width), kind)] * 3
        + [
            pltpu.VMEM((BR * width, BK * width), kind) for _ in range(TICKS)
        ]
        + [
            pltpu.VMEM((BK * width, BC * width), kind),
            pltpu.VMEM((BR * width, BC * width), jnp.float32),
            pltpu.SMEM(a_ids.shape, jnp.int32),
            pltpu.SMEM(a_count.shape, jnp.int32),
            pltpu.SMEM(b_ids.shape, jnp.int32),
            pltpu.SMEM(b_count.shape, jnp.int32),
            pltpu.SMEM((2 * TICKS - 1, 8, 128), jnp.int32),
            dma((4, 4)), dma((3, 4)), dma((6,)), dma((3, 3)), dma((6,)), dma((7,)), dma((96,)),
        ],
        compiler_params=pltpu.CompilerParams(
            collective_id=0, has_side_effects=True, vmem_limit_bytes=60 * 1024 * 1024
        ),
        cost_estimate=pl.CostEstimate(
            flops=2 * BR * width * BC * width * TICKS * BK * width, bytes_accessed=5 * 1024 * 1024, transcendentals=0
        ),
    )(a_blocks, a_ids, a_count, b_blocks, b_ids, b_count)


def solution(mesh):
    return jax.shard_map(
        functools.partial(shards, mesh.shape["row"], mesh.shape["col"]),
        mesh=mesh,
        in_specs=(
            P("row", "col", None),
            P("row", "col"),
            P("row", "col"),
            P("row", "col", None),
            P("row", "col"),
            P("row", "col"),
        ),
        out_specs=P("row", "col"),
        check_vma=False,
    )
```

```python
import functools

import jax
import jax.numpy as jnp
from jax import lax
from jax.experimental import pallas as pl
from jax.experimental.pallas import tpu as pltpu
from jax.sharding import PartitionSpec as P

BR = 8
BK = 4
BC = 8
TICKS = 4
LANES = 8
MESH = pl.DeviceIdType.MESH


def fill(dense, blocks, place, rows, cols):
    width = blocks.shape[-1]
    for number in range(rows * cols):
        r, c = number // cols, number % cols
        slot = place(number)
        block = blocks[jnp.maximum(slot - 1, 0)]
        block = jnp.where(slot > 0, block, jnp.zeros_like(block))
        dense[r * width : (r + 1) * width, c * width : (c + 1) * width] = block


def kernel(
    n_row, n_col, a, a_ids, a_count, b, b_ids, b_count, out,
    own_a, own_b, ra0, ra1, ra2, ra3, rb0, rb1, rb2, meta, ra_meta, rb_meta, lane_in, lane_mid, lane_out, left0, left1, left2, left3, right, total,
    ids_a, count_a, ids_b, count_b, slot_of,
    sem_a, sem_b, sem_m, sem_l, local_sems, meta_sems, send_sems,
):
    ra, rb = (ra0, ra1, ra2, ra3), (rb0, rb1, rb2)
    i, j = lax.axis_index("row"), lax.axis_index("col")
    n_zlo = n_col // 4
    n_z = n_row // LANES * n_zlo
    hop = n_z // 4
    zh, lane = i // LANES, i % LANES
    x, core = lane // 2, lane % 2
    zl, y = j // 4, j % 4
    z = zh * n_zlo + zl
    slots = a.shape[0]
    width = a.shape[-1]
    pieces = 4
    part = slots // pieces
    share = slots // LANES

    locals_ = [
        pltpu.make_async_copy(a_ids, ids_a, local_sems.at[0]),
        pltpu.make_async_copy(a_count, count_a, local_sems.at[1]),
        pltpu.make_async_copy(b_ids, ids_b, local_sems.at[2]),
        pltpu.make_async_copy(b_count, count_b, local_sems.at[3]),
        pltpu.make_async_copy(a, own_a, local_sems.at[4]),
        pltpu.make_async_copy(b.at[pl.ds(0, slots)], own_b, local_sems.at[5]),
    ]
    for copy in locals_:
        copy.start()

    def along_z(steps):
        there = (z + steps + n_z) % n_z
        return ((there // n_zlo) * LANES + lane, (there % n_zlo) * 4 + y)

    barrier = pltpu.get_barrier_semaphore()
    away = hop * (1 - 2 * core)
    senders = [(zh * LANES + (lane + d) % LANES, j) for d in range(1, LANES)]
    senders += [((i + t) % n_row, j) for t in range(1, TICKS)]
    senders += [(i, (j + t) % n_col) for t in range(1, TICKS + 1)]
    senders += [(i, zl * 4 + (y + 1) % 4), (i, zl * 4 + (y + 3) % 4)]
    senders += [along_z(-away)]
    for sender in senders:
        pl.semaphore_signal(barrier, inc=1, device_id=sender, device_id_type=MESH)
    for copy in locals_[:4]:
        copy.wait()
    at_row = lax.broadcasted_iota(jnp.int32, meta.shape, 0)
    at_lane = lax.broadcasted_iota(jnp.int32, meta.shape, 1)
    found = jnp.zeros(meta.shape, jnp.int32)
    for s in range(slots):
        name = jnp.where(s < count_a[0, 0], ids_a[0, s], -1)
        found = jnp.where((at_row == 0) & (at_lane == name), s + 1, found)
        for h in range(2):
            name = jnp.where(s < count_b[0, h], ids_b[0, h * slots + s], -1)
            found = jnp.where((at_row == 1 + h) & (at_lane == name), s + 1, found)
    meta[...] = found
    mine_at = pltpu.make_async_copy(meta, slot_of.at[0], meta_sems.at[0])
    mine_at.start()
    pl.semaphore_wait(barrier, len(senders))

    pending = []

    def send(src, dst, sem, device, slot):
        return pltpu.make_async_remote_copy(
            src_ref=src, dst_ref=dst, send_sem=send_sems.at[slot], recv_sem=sem,
            device_id=device, device_id_type=MESH,
        )

    def start(cond, make):
        slot = len(pending)
        pending.append((cond, functools.partial(make, slot)))
        if cond is None:
            make(slot).start()
        else:
            pl.when(cond)(lambda: make(slot).start())

    def arrived(ref, sem):
        pltpu.make_async_copy(ref, ref, sem).wait()

    def pa(slot, k):
        return ra[slot].at[pl.ds(k * part, part)]

    def pb(slot, k):
        return rb[slot].at[pl.ds(k * part, part)]

    base = slots * (1 - zh)

    @pl.when(lane < 3)
    def _():
        pltpu.make_async_copy(
            b.at[pl.ds(base + share * lane, share)], lane_in.at[lane], sem_l.at[0, lane]
        ).start()

    for d in range(1, LANES):
        to = (lane + d) % LANES
        start(
            lane < 3,
            lambda s, to=to: send(
                b.at[pl.ds(base + share * to, share)], lane_in.at[lane], sem_l.at[0, lane], (zh * LANES + to, j), s
            ),
        )

    up = (y + 2) // 3
    far = (i, (zl - 1 + y // 3 + n_zlo) % n_zlo * 4 + (y + up) % 4)

    def start_far(k):
        mine = a.at[pl.ds(k * part, part)]
        start(y == 0, lambda s: send(mine, pa(3, k), sem_a.at[3, k], far, s))
        start(y > 0, lambda s: send(mine, pa(2, k), sem_a.at[2, k], far, s))

    for k in range(pieces):
        start_far(k)
        mine = a.at[pl.ds(k * part, part)]
        start(y > 0, lambda s, k=k, mine=mine: send(mine, pa(0, k), sem_a.at[0, k], (i, j - 1), s))
        own = b.at[pl.ds(k * part, part)]
        start(x > 0, lambda s, k=k, own=own: send(own, pb(1, k), sem_b.at[1, k], (i - 2, j), s))
        start(core == 1, lambda s, k=k, own=own: send(own, pb(0, k), sem_b.at[0, k], (i - 1, j), s))

    for t in range(1, TICKS):
        start(None, lambda s, t=t: send(meta, ra_meta.at[t - 1], sem_m.at[t - 1], (i, (j - t + n_col) % n_col), s))
        start(None, lambda s, t=t: send(meta, rb_meta.at[t - 1], sem_m.at[t + 2], ((i - t + n_row) % n_row, j), s))
    mine_at.wait()
    for copy in locals_[4:]:
        copy.wait()

    tile = 2 * width

    lefts = (left0, left1, left2, left3)

    def expand_left(t, a_panel):
        fill(lefts[t], a_panel, lambda n: slot_of[t, 0, n], BR, BK)

    def add_tick(t, b_at, half, b_panel):
        left = lefts[t]
        fill(right, b_panel, lambda n: slot_of[b_at, 1 + half, n], BK, BC)

        @pl.loop(0, BR * width // tile)
        def _(step):
            rows = pl.ds(pl.multiple_of(step * tile, tile), tile)
            product = jnp.dot(left[rows, :], right[...], preferred_element_type=jnp.float32)
            if t > 0:
                product = total[rows, :] + product
            if t < TICKS - 1:
                total[rows, :] = product
            else:
                out[rows, :] = product.astype(out.dtype)

    expand_left(0, own_a)
    add_tick(0, 0, 0, own_b)

    def lanes_first(p):
        arrived(lane_in.at[p], sem_l.at[0, p])
        start(None, lambda s: send(lane_in.at[p], lane_mid.at[p], sem_l.at[1, p], along_z(away), s))

    def lanes_second(p):
        arrived(lane_mid.at[p], sem_l.at[1, p])
        start(None, lambda s: send(lane_mid.at[p], lane_out.at[p], sem_l.at[2, p], along_z(away), s))

    def lanes_last(p):
        arrived(lane_out.at[p], sem_l.at[2, p])
        for goal, slot in (((6, 1), (5, 2)), ((7, 1),), ((7, 2),))[p]:
            into = rb[slot].at[pl.ds(lane * share, share)]
            sem = sem_b.at[slot, lane // 2]

            @pl.when(lane == goal)
            def _():
                pltpu.make_async_copy(lane_out.at[p], into, sem).start()

            start(
                lane != goal,
                lambda s, goal=goal, into=into, sem=sem: send(lane_out.at[p], into, sem, (zh * LANES + goal, j), s),
            )

    def near(to):
        return (i, zl * 4 + to)

    def forward_first(k):
        low = k < pieces // 2

        @pl.when(y == 0)
        def _():
            arrived(pa(3, k), sem_a.at[3, k])

        start(y == 0, lambda s: send(pa(3, k), pa(2, k), sem_a.at[2, k], near(1), s))
        start(y == 0, lambda s: send(pa(3, k), pa(0, k), sem_a.at[0, k], near(3), s))

        @pl.when((y == 1) | (y == 2))
        def _():
            arrived(pa(0, k), sem_a.at[0, k])

        start(y == 1, lambda s: send(pa(0, k), pa(1, k), sem_a.at[1, k], near(0), s))
        if not low:
            start(y == 2, lambda s: send(pa(0, k), pa(1, k), sem_a.at[1, k], near(1), s))

        @pl.when((y == 0) | (y == 2))
        def _():
            arrived(pa(2, k), sem_a.at[2, k])

        start(y == 2, lambda s: send(pa(2, k), pa(1, k), sem_a.at[1, k], near(3), s))
        if low:
            start(y == 0, lambda s: send(pa(2, k), pa(1, k), sem_a.at[1, k], near(1), s))

    def forward_second(k):
        low = k < pieces // 2

        @pl.when(y == 1)
        def _():
            arrived(pa(2, k), sem_a.at[2, k])

        @pl.when(y == 3)
        def _():
            arrived(pa(0, k), sem_a.at[0, k])

        if low:
            start(y == 1, lambda s: send(pa(2, k), pa(1, k), sem_a.at[1, k], near(2), s))
        else:
            start(y == 3, lambda s: send(pa(0, k), pa(1, k), sem_a.at[1, k], near(2), s))

    def forward_b(k, here, back):
        @pl.when(here)
        def _():
            arrived(pb(1, k), sem_b.at[1, k])

        start(here & (core == 0), lambda s: send(pb(1, k), pb(0, k), sem_b.at[0, k], (i + 1, j), s))
        start(back, lambda s: send(pb(1, k), pb(2, k), sem_b.at[2, k], (i - 1, j), s))

    for p in range(3):
        lanes_first(p)
    for k in range(pieces):
        forward_first(k)
        forward_b(k, x < 3, (x < 3) & (lane > 0))
        if k > 0:
            forward_second(k - 1)
            lanes_second(k - 1)
    forward_second(pieces - 1)
    lanes_last(0)

    for t in range(TICKS - 1):
        arrived(ra_meta.at[t], sem_m.at[t])
        arrived(rb_meta.at[t], sem_m.at[t + 3])
    moves = [pltpu.make_async_copy(ra_meta.at[t], slot_of.at[1 + t], meta_sems.at[1 + t]) for t in range(TICKS - 1)]
    moves += [pltpu.make_async_copy(rb_meta.at[t], slot_of.at[4 + t], meta_sems.at[4 + t]) for t in range(TICKS - 1)]
    for move in moves:
        move.start()
    for move in moves:
        move.wait()

    def later_tick(t):
        if t != 2:
            for k in range(pieces):
                arrived(pb(t - 1, k), sem_b.at[t - 1, k])
        add_tick(t, 3 + t, (i + t) // n_row, rb[t - 1])

    for k in range(pieces):
        pl.when(y == 0)(lambda k=k: arrived(pa(0, k), sem_a.at[0, k]))
    expand_left(1, ra[0])
    pl.when(x < 3)(lambda: later_tick(1))
    lanes_last(1)
    for k in range(pieces):
        arrived(pa(1, k), sem_a.at[1, k])
    expand_left(2, ra[1])
    pl.when(x < 3)(lambda: later_tick(2))
    lanes_last(2)
    for k in range(pieces):
        forward_b(k, x == 3, lane == LANES - 1)
    for k in range(pieces):
        pl.when(y == 3)(lambda k=k: arrived(pa(2, k), sem_a.at[2, k]))
    expand_left(3, ra[2])
    pl.when(x == 3)(lambda: later_tick(1))
    pl.when(x == 3)(lambda: later_tick(2))
    later_tick(3)
    for cond, make in pending:
        if cond is None:
            make().wait_send()
        else:
            pl.when(cond)(lambda make=make: make().wait_send())


def shards(n_row, n_col, a_blocks, a_ids, a_count, b_blocks, b_ids, b_count):
    slots = a_blocks.shape[0]
    width = a_blocks.shape[1]
    share = slots // LANES
    kind = a_blocks.dtype
    panel = (slots, width, width)
    hbm = pl.BlockSpec(memory_space=pl.ANY)
    dma = pltpu.SemaphoreType.DMA
    return pl.pallas_call(
        functools.partial(kernel, n_row, n_col),
        out_shape=jax.ShapeDtypeStruct((BR * width, BC * width), kind),
        in_specs=[hbm] * 6,
        out_specs=pl.BlockSpec(memory_space=pltpu.VMEM),
        scratch_shapes=[
            pltpu.VMEM(panel, kind) for _ in range(2 + TICKS + TICKS - 1)
        ]
        + [
            pltpu.VMEM((8, 128), jnp.int32),
            pltpu.VMEM((TICKS - 1, 8, 128), jnp.int32),
            pltpu.VMEM((TICKS - 1, 8, 128), jnp.int32),
        ]
        + [pltpu.VMEM((3, share, width, width), kind)] * 3
        + [
            pltpu.VMEM((BR * width, BK * width), kind) for _ in range(TICKS)
        ]
        + [
            pltpu.VMEM((BK * width, BC * width), kind),
            pltpu.VMEM((BR * width, BC * width), jnp.float32),
            pltpu.SMEM(a_ids.shape, jnp.int32),
            pltpu.SMEM(a_count.shape, jnp.int32),
            pltpu.SMEM(b_ids.shape, jnp.int32),
            pltpu.SMEM(b_count.shape, jnp.int32),
            pltpu.SMEM((2 * TICKS - 1, 8, 128), jnp.int32),
            dma((4, 4)), dma((3, 4)), dma((6,)), dma((3, 3)), dma((6,)), dma((7,)), dma((96,)),
        ],
        compiler_params=pltpu.CompilerParams(
            collective_id=0, has_side_effects=True, vmem_limit_bytes=60 * 1024 * 1024
        ),
        cost_estimate=pl.CostEstimate(
            flops=2 * BR * width * BC * width * TICKS * BK * width, bytes_accessed=5 * 1024 * 1024, transcendentals=0
        ),
    )(a_blocks, a_ids, a_count, b_blocks, b_ids, b_count)


def solution(mesh):
    return jax.shard_map(
        functools.partial(shards, mesh.shape["row"], mesh.shape["col"]),
        mesh=mesh,
        in_specs=(
            P("row", "col", None),
            P("row", "col"),
            P("row", "col"),
            P("row", "col", None),
            P("row", "col"),
            P("row", "col"),
        ),
        out_specs=P("row", "col"),
        check_vma=False,
    )
```

```python
import functools

import jax
import jax.numpy as jnp
from jax import lax
from jax.experimental import pallas as pl
from jax.experimental.pallas import tpu as pltpu
from jax.sharding import PartitionSpec as P

BR = 8
BK = 4
BC = 8
TICKS = 4
LANES = 8
MESH = pl.DeviceIdType.MESH


def fill(dense, blocks, place, rows, cols):
    width = blocks.shape[-1]
    for number in range(rows * cols):
        r, c = number // cols, number % cols
        slot = place(number)
        block = blocks[jnp.maximum(slot - 1, 0)]
        block = jnp.where(slot > 0, block, jnp.zeros_like(block))
        dense[r * width : (r + 1) * width, c * width : (c + 1) * width] = block


def kernel(
    n_row, n_col, a, a_ids, a_count, b, b_ids, b_count, out,
    own_a, own_b, ra0, ra1, ra2, ra3, rb0, rb1, rb2, meta, ra_meta, rb_meta, lane_in, lane_mid, lane_out, left0, left1, left2, left3, right, total,
    ids_a, count_a, ids_b, count_b, slot_of,
    sem_a, sem_b, sem_m, sem_l, local_sems, meta_sems, send_sems,
):
    ra, rb = (ra0, ra1, ra2, ra3), (rb0, rb1, rb2)
    i, j = lax.axis_index("row"), lax.axis_index("col")
    n_zlo = n_col // 4
    n_z = n_row // LANES * n_zlo
    hop = n_z // 4
    zh, lane = i // LANES, i % LANES
    x, core = lane // 2, lane % 2
    zl, y = j // 4, j % 4
    z = zh * n_zlo + zl
    slots = a.shape[0]
    width = a.shape[-1]
    pieces = 4
    part = slots // pieces
    share = slots // LANES

    locals_ = [
        pltpu.make_async_copy(a_ids, ids_a, local_sems.at[0]),
        pltpu.make_async_copy(a_count, count_a, local_sems.at[1]),
        pltpu.make_async_copy(b_ids, ids_b, local_sems.at[2]),
        pltpu.make_async_copy(b_count, count_b, local_sems.at[3]),
        pltpu.make_async_copy(a, own_a, local_sems.at[4]),
        pltpu.make_async_copy(b.at[pl.ds(0, slots)], own_b, local_sems.at[5]),
    ]
    for copy in locals_:
        copy.start()

    def along_z(steps):
        there = (z + steps + n_z) % n_z
        return ((there // n_zlo) * LANES + lane, (there % n_zlo) * 4 + y)

    barrier = pltpu.get_barrier_semaphore()
    away = hop * (1 - 2 * core)
    senders = [(zh * LANES + (lane + d) % LANES, j) for d in range(1, LANES)]
    senders += [((i + t) % n_row, j) for t in range(1, TICKS)]
    senders += [(i, (j + t) % n_col) for t in range(1, TICKS + 1)]
    senders += [(i, zl * 4 + (y + 1) % 4), (i, zl * 4 + (y + 3) % 4)]
    senders += [along_z(-away)]
    for sender in senders:
        pl.semaphore_signal(barrier, inc=1, device_id=sender, device_id_type=MESH)
    for copy in locals_[:4]:
        copy.wait()
    at_row = lax.broadcasted_iota(jnp.int32, meta.shape, 0)
    at_lane = lax.broadcasted_iota(jnp.int32, meta.shape, 1)
    found = jnp.zeros(meta.shape, jnp.int32)
    for s in range(slots):
        name = jnp.where(s < count_a[0, 0], ids_a[0, s], -1)
        found = jnp.where((at_row == 0) & (at_lane == name), s + 1, found)
        for h in range(2):
            name = jnp.where(s < count_b[0, h], ids_b[0, h * slots + s], -1)
            found = jnp.where((at_row == 1 + h) & (at_lane == name), s + 1, found)
    meta[...] = found
    mine_at = pltpu.make_async_copy(meta, slot_of.at[0], meta_sems.at[0])
    mine_at.start()
    pl.semaphore_wait(barrier, len(senders))

    pending = []

    def send(src, dst, sem, device, slot):
        return pltpu.make_async_remote_copy(
            src_ref=src, dst_ref=dst, send_sem=send_sems.at[slot], recv_sem=sem,
            device_id=device, device_id_type=MESH,
        )

    def start(cond, make):
        slot = len(pending)
        pending.append((cond, functools.partial(make, slot)))
        if cond is None:
            make(slot).start()
        else:
            pl.when(cond)(lambda: make(slot).start())

    def arrived(ref, sem):
        pltpu.make_async_copy(ref, ref, sem).wait()

    def pa(slot, k):
        return ra[slot].at[pl.ds(k * part, part)]

    def pb(slot, k):
        return rb[slot].at[pl.ds(k * part, part)]

    base = slots * (1 - zh)

    @pl.when(lane < 3)
    def _():
        pltpu.make_async_copy(
            b.at[pl.ds(base + share * lane, share)], lane_in.at[lane], sem_l.at[0, lane]
        ).start()

    for d in range(1, LANES):
        to = (lane + d) % LANES
        start(
            lane < 3,
            lambda s, to=to: send(
                b.at[pl.ds(base + share * to, share)], lane_in.at[lane], sem_l.at[0, lane], (zh * LANES + to, j), s
            ),
        )

    up = (y + 2) // 3
    far = (i, (zl - 1 + y // 3 + n_zlo) % n_zlo * 4 + (y + up) % 4)

    def start_far(k):
        mine = a.at[pl.ds(k * part, part)]
        start(y == 0, lambda s: send(mine, pa(3, k), sem_a.at[3, k], far, s))
        start(y > 0, lambda s: send(mine, pa(2, k), sem_a.at[2, k], far, s))

    for k in range(pieces):
        start_far(k)
        mine = a.at[pl.ds(k * part, part)]
        start(y > 0, lambda s, k=k, mine=mine: send(mine, pa(0, k), sem_a.at[0, k], (i, j - 1), s))
        own = b.at[pl.ds(k * part, part)]
        start(x > 0, lambda s, k=k, own=own: send(own, pb(1, k), sem_b.at[1, k], (i - 2, j), s))
        start(core == 1, lambda s, k=k, own=own: send(own, pb(0, k), sem_b.at[0, k], (i - 1, j), s))

    for t in range(1, TICKS):
        start(None, lambda s, t=t: send(meta, ra_meta.at[t - 1], sem_m.at[t - 1], (i, (j - t + n_col) % n_col), s))
        start(None, lambda s, t=t: send(meta, rb_meta.at[t - 1], sem_m.at[t + 2], ((i - t + n_row) % n_row, j), s))
    mine_at.wait()
    for copy in locals_[4:]:
        copy.wait()

    tile = 2 * width

    lefts = (left0, left1, left2, left3)

    def expand_left(t, a_panel):
        fill(lefts[t], a_panel, lambda n: slot_of[t, 0, n], BR, BK)

    def add_tick(t, b_at, half, b_panel):
        left = lefts[t]
        fill(right, b_panel, lambda n: slot_of[b_at, 1 + half, n], BK, BC)

        @pl.loop(0, BR * width // tile)
        def _(step):
            rows = pl.ds(pl.multiple_of(step * tile, tile), tile)
            product = jnp.dot(left[rows, :], right[...], preferred_element_type=jnp.float32)
            if t > 0:
                product = total[rows, :] + product
            if t < TICKS - 1:
                total[rows, :] = product
            else:
                out[rows, :] = product.astype(out.dtype)

    expand_left(0, own_a)
    add_tick(0, 0, 0, own_b)

    def lanes_first(p):
        arrived(lane_in.at[p], sem_l.at[0, p])
        start(None, lambda s: send(lane_in.at[p], lane_mid.at[p], sem_l.at[1, p], along_z(away), s))

    def lanes_second(p):
        arrived(lane_mid.at[p], sem_l.at[1, p])
        start(None, lambda s: send(lane_mid.at[p], lane_out.at[p], sem_l.at[2, p], along_z(away), s))

    def lanes_last(p):
        arrived(lane_out.at[p], sem_l.at[2, p])
        for goal, slot in (((6, 1), (5, 2)), ((7, 1),), ((7, 2),))[p]:
            into = rb[slot].at[pl.ds(lane * share, share)]
            sem = sem_b.at[slot, lane // 2]

            @pl.when(lane == goal)
            def _():
                pltpu.make_async_copy(lane_out.at[p], into, sem).start()

            start(
                lane != goal,
                lambda s, goal=goal, into=into, sem=sem: send(lane_out.at[p], into, sem, (zh * LANES + goal, j), s),
            )

    def near(to):
        return (i, zl * 4 + to)

    def forward_first(k):
        low = k < pieces // 2

        @pl.when(y == 0)
        def _():
            arrived(pa(3, k), sem_a.at[3, k])

        start(y == 0, lambda s: send(pa(3, k), pa(2, k), sem_a.at[2, k], near(1), s))
        start(y == 0, lambda s: send(pa(3, k), pa(0, k), sem_a.at[0, k], near(3), s))

        @pl.when((y == 1) | (y == 2))
        def _():
            arrived(pa(0, k), sem_a.at[0, k])

        start(y == 1, lambda s: send(pa(0, k), pa(1, k), sem_a.at[1, k], near(0), s))
        if not low:
            start(y == 2, lambda s: send(pa(0, k), pa(1, k), sem_a.at[1, k], near(1), s))

        @pl.when((y == 0) | (y == 2))
        def _():
            arrived(pa(2, k), sem_a.at[2, k])

        start(y == 2, lambda s: send(pa(2, k), pa(1, k), sem_a.at[1, k], near(3), s))
        if low:
            start(y == 0, lambda s: send(pa(2, k), pa(1, k), sem_a.at[1, k], near(1), s))

    def forward_second(k):
        low = k < pieces // 2

        @pl.when(y == 1)
        def _():
            arrived(pa(2, k), sem_a.at[2, k])

        @pl.when(y == 3)
        def _():
            arrived(pa(0, k), sem_a.at[0, k])

        if low:
            start(y == 1, lambda s: send(pa(2, k), pa(1, k), sem_a.at[1, k], near(2), s))
        else:
            start(y == 3, lambda s: send(pa(0, k), pa(1, k), sem_a.at[1, k], near(2), s))

    def forward_b(k, here, back):
        @pl.when(here)
        def _():
            arrived(pb(1, k), sem_b.at[1, k])

        start(here & (core == 0), lambda s: send(pb(1, k), pb(0, k), sem_b.at[0, k], (i + 1, j), s))
        if back is not None:
            start(back, lambda s: send(pb(1, k), pb(2, k), sem_b.at[2, k], (i - 1, j), s))

    lanes_first(0)
    for k in range(pieces):
        forward_first(k)
        forward_b(k, x < 3, (x < 3) & (lane > 0))
        if k > 0:
            forward_second(k - 1)
        if 0 < k < 3:
            lanes_second(k - 1)
        if k < 2:
            lanes_first(k + 1)
    lanes_last(0)
    lanes_second(2)
    forward_second(pieces - 1)

    for t in range(TICKS - 1):
        arrived(ra_meta.at[t], sem_m.at[t])
        arrived(rb_meta.at[t], sem_m.at[t + 3])
    moves = [pltpu.make_async_copy(ra_meta.at[t], slot_of.at[1 + t], meta_sems.at[1 + t]) for t in range(TICKS - 1)]
    moves += [pltpu.make_async_copy(rb_meta.at[t], slot_of.at[4 + t], meta_sems.at[4 + t]) for t in range(TICKS - 1)]
    for move in moves:
        move.start()
    for move in moves:
        move.wait()

    def later_tick(t):
        if t != 2:
            for k in range(pieces):
                arrived(pb(t - 1, k), sem_b.at[t - 1, k])
        add_tick(t, 3 + t, (i + t) // n_row, rb[t - 1])

    for k in range(pieces):
        pl.when(y == 0)(lambda k=k: arrived(pa(0, k), sem_a.at[0, k]))
    expand_left(1, ra[0])
    pl.when(lane < LANES - 1)(lambda: later_tick(1))
    lanes_last(1)
    for k in range(pieces):
        arrived(pa(1, k), sem_a.at[1, k])
    expand_left(2, ra[1])
    pl.when(x < 3)(lambda: later_tick(2))
    for k in range(pieces):
        forward_b(k, lane == LANES - 2, None)
    lanes_last(2)
    for k in range(pieces):
        forward_b(k, lane == LANES - 1, lane == LANES - 1)
    for k in range(pieces):
        pl.when(y == 3)(lambda k=k: arrived(pa(2, k), sem_a.at[2, k]))
    expand_left(3, ra[2])
    pl.when(lane == LANES - 1)(lambda: later_tick(1))
    pl.when(x == 3)(lambda: later_tick(2))
    later_tick(3)
    for cond, make in pending:
        if cond is None:
            make().wait_send()
        else:
            pl.when(cond)(lambda make=make: make().wait_send())


def shards(n_row, n_col, a_blocks, a_ids, a_count, b_blocks, b_ids, b_count):
    slots = a_blocks.shape[0]
    width = a_blocks.shape[1]
    share = slots // LANES
    kind = a_blocks.dtype
    panel = (slots, width, width)
    hbm = pl.BlockSpec(memory_space=pl.ANY)
    dma = pltpu.SemaphoreType.DMA
    return pl.pallas_call(
        functools.partial(kernel, n_row, n_col),
        out_shape=jax.ShapeDtypeStruct((BR * width, BC * width), kind),
        in_specs=[hbm] * 6,
        out_specs=pl.BlockSpec(memory_space=pltpu.VMEM),
        scratch_shapes=[
            pltpu.VMEM(panel, kind) for _ in range(2 + TICKS + TICKS - 1)
        ]
        + [
            pltpu.VMEM((8, 128), jnp.int32),
            pltpu.VMEM((TICKS - 1, 8, 128), jnp.int32),
            pltpu.VMEM((TICKS - 1, 8, 128), jnp.int32),
        ]
        + [pltpu.VMEM((3, share, width, width), kind)] * 3
        + [
            pltpu.VMEM((BR * width, BK * width), kind) for _ in range(TICKS)
        ]
        + [
            pltpu.VMEM((BK * width, BC * width), kind),
            pltpu.VMEM((BR * width, BC * width), jnp.float32),
            pltpu.SMEM(a_ids.shape, jnp.int32),
            pltpu.SMEM(a_count.shape, jnp.int32),
            pltpu.SMEM(b_ids.shape, jnp.int32),
            pltpu.SMEM(b_count.shape, jnp.int32),
            pltpu.SMEM((2 * TICKS - 1, 8, 128), jnp.int32),
            dma((4, 4)), dma((3, 4)), dma((6,)), dma((3, 3)), dma((6,)), dma((7,)), dma((112,)),
        ],
        compiler_params=pltpu.CompilerParams(
            collective_id=0, has_side_effects=True, vmem_limit_bytes=60 * 1024 * 1024
        ),
        cost_estimate=pl.CostEstimate(
            flops=2 * BR * width * BC * width * TICKS * BK * width, bytes_accessed=5 * 1024 * 1024, transcendentals=0
        ),
    )(a_blocks, a_ids, a_count, b_blocks, b_ids, b_count)


def solution(mesh):
    return jax.shard_map(
        functools.partial(shards, mesh.shape["row"], mesh.shape["col"]),
        mesh=mesh,
        in_specs=(
            P("row", "col", None),
            P("row", "col"),
            P("row", "col"),
            P("row", "col", None),
            P("row", "col"),
            P("row", "col"),
        ),
        out_specs=P("row", "col"),
        check_vma=False,
    )
```

```python
import functools

import jax
import jax.numpy as jnp
from jax import lax
from jax.experimental import pallas as pl
from jax.experimental.pallas import tpu as pltpu
from jax.sharding import PartitionSpec as P

BR = 8
BK = 4
BC = 8
TICKS = 4
LANES = 8
MESH = pl.DeviceIdType.MESH


def fill(dense, blocks, place, rows, cols):
    width = blocks.shape[-1]
    for number in range(rows * cols):
        r, c = number // cols, number % cols
        slot = place(number)
        block = blocks[jnp.maximum(slot - 1, 0)]
        block = jnp.where(slot > 0, block, jnp.zeros_like(block))
        dense[r * width : (r + 1) * width, c * width : (c + 1) * width] = block


def kernel(
    n_row, n_col, a, a_ids, a_count, b, b_ids, b_count, out,
    own_a, own_b, ra0, ra1, ra2, ra3, rb0, rb1, rb2, meta, ra_meta, rb_meta, lane_in, lane_mid, lane_out, left0, left1, left2, left3, right, total,
    ids_a, count_a, ids_b, count_b, slot_of,
    sem_a, sem_b, sem_m, sem_l, local_sems, meta_sems, send_sems,
):
    ra, rb = (ra0, ra1, ra2, ra3), (rb0, rb1, rb2)
    i, j = lax.axis_index("row"), lax.axis_index("col")
    n_zlo = n_col // 4
    n_z = n_row // LANES * n_zlo
    hop = n_z // 4
    zh, lane = i // LANES, i % LANES
    x, core = lane // 2, lane % 2
    zl, y = j // 4, j % 4
    z = zh * n_zlo + zl
    slots = a.shape[0]
    width = a.shape[-1]
    pieces = 4
    part = slots // pieces
    share = slots // LANES

    locals_ = [
        pltpu.make_async_copy(a_ids, ids_a, local_sems.at[0]),
        pltpu.make_async_copy(a_count, count_a, local_sems.at[1]),
        pltpu.make_async_copy(b_ids, ids_b, local_sems.at[2]),
        pltpu.make_async_copy(b_count, count_b, local_sems.at[3]),
        pltpu.make_async_copy(a, own_a, local_sems.at[4]),
        pltpu.make_async_copy(b.at[pl.ds(0, slots)], own_b, local_sems.at[5]),
    ]
    for copy in locals_:
        copy.start()

    def along_z(steps):
        there = (z + steps + n_z) % n_z
        return ((there // n_zlo) * LANES + lane, (there % n_zlo) * 4 + y)

    barrier = pltpu.get_barrier_semaphore()
    away = hop * (1 - 2 * core)
    senders = [(zh * LANES + (lane + d) % LANES, j) for d in range(1, LANES)]
    senders += [((i + t) % n_row, j) for t in range(1, TICKS)]
    senders += [(i, (j + t) % n_col) for t in range(1, TICKS + 1)]
    senders += [(i, zl * 4 + (y + 1) % 4), (i, zl * 4 + (y + 3) % 4)]
    senders += [along_z(-away)]
    for sender in senders:
        pl.semaphore_signal(barrier, inc=1, device_id=sender, device_id_type=MESH)
    pl.semaphore_wait(barrier, len(senders))

    pending = []

    def send(src, dst, sem, device, slot):
        return pltpu.make_async_remote_copy(
            src_ref=src, dst_ref=dst, send_sem=send_sems.at[slot], recv_sem=sem,
            device_id=device, device_id_type=MESH,
        )

    def start(cond, make):
        slot = len(pending)
        pending.append((cond, functools.partial(make, slot)))
        if cond is None:
            make(slot).start()
        else:
            pl.when(cond)(lambda: make(slot).start())

    def arrived(ref, sem):
        pltpu.make_async_copy(ref, ref, sem).wait()

    def pa(slot, k):
        return ra[slot].at[pl.ds(k * part, part)]

    def pb(slot, k):
        return rb[slot].at[pl.ds(k * part, part)]

    base = slots * (1 - zh)

    @pl.when(lane < 3)
    def _():
        pltpu.make_async_copy(
            b.at[pl.ds(base + share * lane, share)], lane_in.at[lane], sem_l.at[0, lane]
        ).start()

    for d in range(1, LANES):
        to = (lane + d) % LANES
        start(
            lane < 3,
            lambda s, to=to: send(
                b.at[pl.ds(base + share * to, share)], lane_in.at[lane], sem_l.at[0, lane], (zh * LANES + to, j), s
            ),
        )

    up = (y + 2) // 3
    far = (i, (zl - 1 + y // 3 + n_zlo) % n_zlo * 4 + (y + up) % 4)

    def start_far(k):
        mine = a.at[pl.ds(k * part, part)]
        start(y == 0, lambda s: send(mine, pa(3, k), sem_a.at[3, k], far, s))
        start(y > 0, lambda s: send(mine, pa(2, k), sem_a.at[2, k], far, s))

    for k in range(pieces):
        start_far(k)
        mine = a.at[pl.ds(k * part, part)]
        start(y > 0, lambda s, k=k, mine=mine: send(mine, pa(0, k), sem_a.at[0, k], (i, j - 1), s))
        own = b.at[pl.ds(k * part, part)]
        start(x > 0, lambda s, k=k, own=own: send(own, pb(1, k), sem_b.at[1, k], (i - 2, j), s))
        start(core == 1, lambda s, k=k, own=own: send(own, pb(0, k), sem_b.at[0, k], (i - 1, j), s))

    for copy in locals_[:4]:
        copy.wait()
    at_row = lax.broadcasted_iota(jnp.int32, meta.shape, 0)
    at_lane = lax.broadcasted_iota(jnp.int32, meta.shape, 1)
    found = jnp.zeros(meta.shape, jnp.int32)
    for s in range(slots):
        name = jnp.where(s < count_a[0, 0], ids_a[0, s], -1)
        found = jnp.where((at_row == 0) & (at_lane == name), s + 1, found)
        for h in range(2):
            name = jnp.where(s < count_b[0, h], ids_b[0, h * slots + s], -1)
            found = jnp.where((at_row == 1 + h) & (at_lane == name), s + 1, found)
    meta[...] = found
    mine_at = pltpu.make_async_copy(meta, slot_of.at[0], meta_sems.at[0])
    mine_at.start()
    for t in range(1, TICKS):
        start(None, lambda s, t=t: send(meta, ra_meta.at[t - 1], sem_m.at[t - 1], (i, (j - t + n_col) % n_col), s))
        start(None, lambda s, t=t: send(meta, rb_meta.at[t - 1], sem_m.at[t + 2], ((i - t + n_row) % n_row, j), s))

    tile = 2 * width

    lefts = (left0, left1, left2, left3)

    def expand_left(t, a_panel):
        fill(lefts[t], a_panel, lambda n: slot_of[t, 0, n], BR, BK)

    def add_tick(t, b_at, half, b_panel):
        left = lefts[t]
        fill(right, b_panel, lambda n: slot_of[b_at, 1 + half, n], BK, BC)

        @pl.loop(0, BR * width // tile)
        def _(step):
            rows = pl.ds(pl.multiple_of(step * tile, tile), tile)
            product = jnp.dot(left[rows, :], right[...], preferred_element_type=jnp.float32)
            if t > 0:
                product = total[rows, :] + product
            if t < TICKS - 1:
                total[rows, :] = product
            else:
                out[rows, :] = product.astype(out.dtype)

    def first_tick():
        mine_at.wait()
        for copy in locals_[4:]:
            copy.wait()
        expand_left(0, own_a)
        add_tick(0, 0, 0, own_b)

    def lanes_first(p):
        arrived(lane_in.at[p], sem_l.at[0, p])
        start(None, lambda s: send(lane_in.at[p], lane_mid.at[p], sem_l.at[1, p], along_z(away), s))

    def lanes_second(p):
        arrived(lane_mid.at[p], sem_l.at[1, p])
        start(None, lambda s: send(lane_mid.at[p], lane_out.at[p], sem_l.at[2, p], along_z(away), s))

    def lanes_last(p):
        arrived(lane_out.at[p], sem_l.at[2, p])
        for goal, slot in (((6, 1), (5, 2)), ((7, 1),), ((7, 2),))[p]:
            into = rb[slot].at[pl.ds(lane * share, share)]
            sem = sem_b.at[slot, lane // 2]

            @pl.when(lane == goal)
            def _():
                pltpu.make_async_copy(lane_out.at[p], into, sem).start()

            start(
                lane != goal,
                lambda s, goal=goal, into=into, sem=sem: send(lane_out.at[p], into, sem, (zh * LANES + goal, j), s),
            )

    def near(to):
        return (i, zl * 4 + to)

    def forward_first(k):
        low = k < pieces // 2

        @pl.when(y == 0)
        def _():
            arrived(pa(3, k), sem_a.at[3, k])

        start(y == 0, lambda s: send(pa(3, k), pa(2, k), sem_a.at[2, k], near(1), s))
        start(y == 0, lambda s: send(pa(3, k), pa(0, k), sem_a.at[0, k], near(3), s))

        @pl.when((y == 1) | (y == 2))
        def _():
            arrived(pa(0, k), sem_a.at[0, k])

        start(y == 1, lambda s: send(pa(0, k), pa(1, k), sem_a.at[1, k], near(0), s))
        if not low:
            start(y == 2, lambda s: send(pa(0, k), pa(1, k), sem_a.at[1, k], near(1), s))

        @pl.when((y == 0) | (y == 2))
        def _():
            arrived(pa(2, k), sem_a.at[2, k])

        start(y == 2, lambda s: send(pa(2, k), pa(1, k), sem_a.at[1, k], near(3), s))
        if low:
            start(y == 0, lambda s: send(pa(2, k), pa(1, k), sem_a.at[1, k], near(1), s))

    def forward_second(k):
        low = k < pieces // 2

        @pl.when(y == 1)
        def _():
            arrived(pa(2, k), sem_a.at[2, k])

        @pl.when(y == 3)
        def _():
            arrived(pa(0, k), sem_a.at[0, k])

        if low:
            start(y == 1, lambda s: send(pa(2, k), pa(1, k), sem_a.at[1, k], near(2), s))
        else:
            start(y == 3, lambda s: send(pa(0, k), pa(1, k), sem_a.at[1, k], near(2), s))

    def forward_b(k, here, back):
        @pl.when(here)
        def _():
            arrived(pb(1, k), sem_b.at[1, k])

        start(here & (core == 0), lambda s: send(pb(1, k), pb(0, k), sem_b.at[0, k], (i + 1, j), s))
        if back is not None:
            start(back, lambda s: send(pb(1, k), pb(2, k), sem_b.at[2, k], (i - 1, j), s))

    lanes_first(0)
    for k in range(pieces):
        forward_first(k)
        forward_b(k, x < 3, (x < 3) & (lane > 0))
        if k > 0:
            forward_second(k - 1)
        if 0 < k < 3:
            lanes_second(k - 1)
        if k < 2:
            lanes_first(k + 1)
        if k == 1:
            first_tick()
    lanes_last(0)
    lanes_second(2)
    forward_second(pieces - 1)

    for t in range(TICKS - 1):
        arrived(ra_meta.at[t], sem_m.at[t])
        arrived(rb_meta.at[t], sem_m.at[t + 3])
    moves = [pltpu.make_async_copy(ra_meta.at[t], slot_of.at[1 + t], meta_sems.at[1 + t]) for t in range(TICKS - 1)]
    moves += [pltpu.make_async_copy(rb_meta.at[t], slot_of.at[4 + t], meta_sems.at[4 + t]) for t in range(TICKS - 1)]
    for move in moves:
        move.start()
    for move in moves:
        move.wait()

    def later_tick(t):
        if t != 2:
            for k in range(pieces):
                arrived(pb(t - 1, k), sem_b.at[t - 1, k])
        add_tick(t, 3 + t, (i + t) // n_row, rb[t - 1])

    for k in range(pieces):
        pl.when(y == 0)(lambda k=k: arrived(pa(0, k), sem_a.at[0, k]))
    expand_left(1, ra[0])
    pl.when(lane < LANES - 1)(lambda: later_tick(1))
    lanes_last(1)
    for k in range(pieces):
        arrived(pa(1, k), sem_a.at[1, k])
    expand_left(2, ra[1])
    pl.when(x < 3)(lambda: later_tick(2))
    for k in range(pieces):
        forward_b(k, lane == LANES - 2, None)
    for k in range(pieces):
        forward_b(k, lane == LANES - 1, lane == LANES - 1)

    @pl.when(lane == LANES - 1)
    def _():
        later_tick(1)
        later_tick(2)

    lanes_last(2)
    for k in range(pieces):
        pl.when(y == 3)(lambda k=k: arrived(pa(2, k), sem_a.at[2, k]))
    expand_left(3, ra[2])
    pl.when(lane == LANES - 2)(lambda: later_tick(2))
    later_tick(3)
    for cond, make in pending:
        if cond is None:
            make().wait_send()
        else:
            pl.when(cond)(lambda make=make: make().wait_send())


def shards(n_row, n_col, a_blocks, a_ids, a_count, b_blocks, b_ids, b_count):
    slots = a_blocks.shape[0]
    width = a_blocks.shape[1]
    share = slots // LANES
    kind = a_blocks.dtype
    panel = (slots, width, width)
    hbm = pl.BlockSpec(memory_space=pl.ANY)
    dma = pltpu.SemaphoreType.DMA
    return pl.pallas_call(
        functools.partial(kernel, n_row, n_col),
        out_shape=jax.ShapeDtypeStruct((BR * width, BC * width), kind),
        in_specs=[hbm] * 6,
        out_specs=pl.BlockSpec(memory_space=pltpu.VMEM),
        scratch_shapes=[
            pltpu.VMEM(panel, kind) for _ in range(2 + TICKS + TICKS - 1)
        ]
        + [
            pltpu.VMEM((8, 128), jnp.int32),
            pltpu.VMEM((TICKS - 1, 8, 128), jnp.int32),
            pltpu.VMEM((TICKS - 1, 8, 128), jnp.int32),
        ]
        + [pltpu.VMEM((3, share, width, width), kind)] * 3
        + [
            pltpu.VMEM((BR * width, BK * width), kind) for _ in range(TICKS)
        ]
        + [
            pltpu.VMEM((BK * width, BC * width), kind),
            pltpu.VMEM((BR * width, BC * width), jnp.float32),
            pltpu.SMEM(a_ids.shape, jnp.int32),
            pltpu.SMEM(a_count.shape, jnp.int32),
            pltpu.SMEM(b_ids.shape, jnp.int32),
            pltpu.SMEM(b_count.shape, jnp.int32),
            pltpu.SMEM((2 * TICKS - 1, 8, 128), jnp.int32),
            dma((4, 4)), dma((3, 4)), dma((6,)), dma((3, 3)), dma((6,)), dma((7,)), dma((112,)),
        ],
        compiler_params=pltpu.CompilerParams(
            collective_id=0, has_side_effects=True, vmem_limit_bytes=60 * 1024 * 1024
        ),
        cost_estimate=pl.CostEstimate(
            flops=2 * BR * width * BC * width * TICKS * BK * width, bytes_accessed=5 * 1024 * 1024, transcendentals=0
        ),
    )(a_blocks, a_ids, a_count, b_blocks, b_ids, b_count)


def solution(mesh):
    return jax.shard_map(
        functools.partial(shards, mesh.shape["row"], mesh.shape["col"]),
        mesh=mesh,
        in_specs=(
            P("row", "col", None),
            P("row", "col"),
            P("row", "col"),
            P("row", "col", None),
            P("row", "col"),
            P("row", "col"),
        ),
        out_specs=P("row", "col"),
        check_vma=False,
    )
```

```python
import functools

import jax
import jax.numpy as jnp
from jax import lax
from jax.experimental import pallas as pl
from jax.experimental.pallas import tpu as pltpu
from jax.sharding import PartitionSpec as P

BR = 8
BK = 4
BC = 8
TICKS = 4
LANES = 8
MESH = pl.DeviceIdType.MESH


def fill(dense, blocks, place, rows, cols):
    width = blocks.shape[-1]
    for number in range(rows * cols):
        r, c = number // cols, number % cols
        slot = place(number)
        block = blocks[jnp.maximum(slot - 1, 0)]
        block = jnp.where(slot > 0, block, jnp.zeros_like(block))
        dense[r * width : (r + 1) * width, c * width : (c + 1) * width] = block


def kernel(
    n_row, n_col, a, a_ids, a_count, b, b_ids, b_count, out,
    own_a, own_b, ra0, ra1, ra2, ra3, rb0, rb1, rb2, meta, ra_meta, rb_meta, lane_in, lane_mid, lane_out, left0, left1, left2, left3, right, total,
    ids_a, count_a, ids_b, count_b, slot_of,
    sem_a, sem_b, sem_m, sem_l, local_sems, meta_sems, send_sems,
):
    ra, rb = (ra0, ra1, ra2, ra3), (rb0, rb1, rb2)
    i, j = lax.axis_index("row"), lax.axis_index("col")
    n_zlo = n_col // 4
    n_z = n_row // LANES * n_zlo
    hop = n_z // 4
    zh, lane = i // LANES, i % LANES
    x, core = lane // 2, lane % 2
    zl, y = j // 4, j % 4
    z = zh * n_zlo + zl
    slots = a.shape[0]
    width = a.shape[-1]
    pieces = 4
    part = slots // pieces
    share = slots // LANES

    locals_ = [
        pltpu.make_async_copy(a_ids, ids_a, local_sems.at[0]),
        pltpu.make_async_copy(a_count, count_a, local_sems.at[1]),
        pltpu.make_async_copy(b_ids, ids_b, local_sems.at[2]),
        pltpu.make_async_copy(b_count, count_b, local_sems.at[3]),
        pltpu.make_async_copy(a, own_a, local_sems.at[4]),
        pltpu.make_async_copy(b.at[pl.ds(0, slots)], own_b, local_sems.at[5]),
    ]
    for copy in locals_:
        copy.start()

    def along_z(steps):
        there = (z + steps + n_z) % n_z
        return ((there // n_zlo) * LANES + lane, (there % n_zlo) * 4 + y)

    barrier = pltpu.get_barrier_semaphore()
    away = hop * (1 - 2 * core)
    senders = [(zh * LANES + (lane + d) % LANES, j) for d in range(1, LANES)]
    senders += [((i + t) % n_row, j) for t in range(1, TICKS)]
    senders += [(i, (j + t) % n_col) for t in range(1, TICKS + 1)]
    senders += [(i, zl * 4 + (y + 1) % 4), (i, zl * 4 + (y + 3) % 4)]
    senders += [along_z(-away)]
    for sender in senders:
        pl.semaphore_signal(barrier, inc=1, device_id=sender, device_id_type=MESH)
    for copy in locals_[:4]:
        copy.wait()
    at_row = lax.broadcasted_iota(jnp.int32, meta.shape, 0)
    at_lane = lax.broadcasted_iota(jnp.int32, meta.shape, 1)
    found = jnp.zeros(meta.shape, jnp.int32)
    for s in range(slots):
        name = jnp.where(s < count_a[0, 0], ids_a[0, s], -1)
        found = jnp.where((at_row == 0) & (at_lane == name), s + 1, found)
        for h in range(2):
            name = jnp.where(s < count_b[0, h], ids_b[0, h * slots + s], -1)
            found = jnp.where((at_row == 1 + h) & (at_lane == name), s + 1, found)
    meta[...] = found
    mine_at = pltpu.make_async_copy(meta, slot_of.at[0], meta_sems.at[0])
    mine_at.start()
    pl.semaphore_wait(barrier, len(senders))

    pending = []

    def send(src, dst, sem, device, slot):
        return pltpu.make_async_remote_copy(
            src_ref=src, dst_ref=dst, send_sem=send_sems.at[slot], recv_sem=sem,
            device_id=device, device_id_type=MESH,
        )

    def start(cond, make):
        slot = len(pending)
        pending.append((cond, functools.partial(make, slot)))
        if cond is None:
            make(slot).start()
        else:
            pl.when(cond)(lambda: make(slot).start())

    def arrived(ref, sem):
        pltpu.make_async_copy(ref, ref, sem).wait()

    def pa(slot, k):
        return ra[slot].at[pl.ds(k * part, part)]

    def pb(slot, k):
        return rb[slot].at[pl.ds(k * part, part)]

    base = slots * (1 - zh)

    @pl.when(lane < 3)
    def _():
        pltpu.make_async_copy(
            b.at[pl.ds(base + share * lane, share)], lane_in.at[lane], sem_l.at[0, lane]
        ).start()

    for d in range(1, LANES):
        to = (lane + d) % LANES
        start(
            lane < 3,
            lambda s, to=to: send(
                b.at[pl.ds(base + share * to, share)], lane_in.at[lane], sem_l.at[0, lane], (zh * LANES + to, j), s
            ),
        )

    up = (y + 2) // 3
    far = (i, (zl - 1 + y // 3 + n_zlo) % n_zlo * 4 + (y + up) % 4)

    def start_far(k):
        mine = a.at[pl.ds(k * part, part)]
        start(y == 0, lambda s: send(mine, pa(3, k), sem_a.at[3, k], far, s))
        start(y > 0, lambda s: send(mine, pa(2, k), sem_a.at[2, k], far, s))

    for k in range(pieces):
        if k < 2:
            start_far(k)
        mine = a.at[pl.ds(k * part, part)]
        start(y > 0, lambda s, k=k, mine=mine: send(mine, pa(0, k), sem_a.at[0, k], (i, j - 1), s))
        own = b.at[pl.ds(k * part, part)]
        start(x > 0, lambda s, k=k, own=own: send(own, pb(1, k), sem_b.at[1, k], (i - 2, j), s))
        start(core == 1, lambda s, k=k, own=own: send(own, pb(0, k), sem_b.at[0, k], (i - 1, j), s))

    for t in range(1, TICKS):
        start(None, lambda s, t=t: send(meta, ra_meta.at[t - 1], sem_m.at[t - 1], (i, (j - t + n_col) % n_col), s))
        start(None, lambda s, t=t: send(meta, rb_meta.at[t - 1], sem_m.at[t + 2], ((i - t + n_row) % n_row, j), s))
    mine_at.wait()
    for copy in locals_[4:]:
        copy.wait()

    tile = 2 * width

    lefts = (left0, left1, left2, left3)

    def expand_left(t, a_panel):
        fill(lefts[t], a_panel, lambda n: slot_of[t, 0, n], BR, BK)

    def add_tick(t, b_at, half, b_panel):
        left = lefts[t]
        fill(right, b_panel, lambda n: slot_of[b_at, 1 + half, n], BK, BC)

        @pl.loop(0, BR * width // tile)
        def _(step):
            rows = pl.ds(pl.multiple_of(step * tile, tile), tile)
            product = jnp.dot(left[rows, :], right[...], preferred_element_type=jnp.float32)
            if t > 0:
                product = total[rows, :] + product
            if t < TICKS - 1:
                total[rows, :] = product
            else:
                out[rows, :] = product.astype(out.dtype)

    expand_left(0, own_a)
    add_tick(0, 0, 0, own_b)

    def lanes_first(p):
        arrived(lane_in.at[p], sem_l.at[0, p])
        start(None, lambda s: send(lane_in.at[p], lane_mid.at[p], sem_l.at[1, p], along_z(away), s))

    def lanes_second(p):
        arrived(lane_mid.at[p], sem_l.at[1, p])
        start(None, lambda s: send(lane_mid.at[p], lane_out.at[p], sem_l.at[2, p], along_z(away), s))

    def lanes_last(p):
        arrived(lane_out.at[p], sem_l.at[2, p])
        for goal, slot in (((6, 1), (5, 2)), ((7, 1),), ((7, 2),))[p]:
            into = rb[slot].at[pl.ds(lane * share, share)]
            sem = sem_b.at[slot, lane // 2]

            @pl.when(lane == goal)
            def _():
                pltpu.make_async_copy(lane_out.at[p], into, sem).start()

            start(
                lane != goal,
                lambda s, goal=goal, into=into, sem=sem: send(lane_out.at[p], into, sem, (zh * LANES + goal, j), s),
            )

    def near(to):
        return (i, zl * 4 + to)

    def forward_first(k):
        low = k < pieces // 2

        @pl.when(y == 0)
        def _():
            arrived(pa(3, k), sem_a.at[3, k])

        start(y == 0, lambda s: send(pa(3, k), pa(2, k), sem_a.at[2, k], near(1), s))
        start(y == 0, lambda s: send(pa(3, k), pa(0, k), sem_a.at[0, k], near(3), s))

        @pl.when((y == 1) | (y == 2))
        def _():
            arrived(pa(0, k), sem_a.at[0, k])

        start(y == 1, lambda s: send(pa(0, k), pa(1, k), sem_a.at[1, k], near(0), s))
        if not low:
            start(y == 2, lambda s: send(pa(0, k), pa(1, k), sem_a.at[1, k], near(1), s))

        @pl.when((y == 0) | (y == 2))
        def _():
            arrived(pa(2, k), sem_a.at[2, k])

        start(y == 2, lambda s: send(pa(2, k), pa(1, k), sem_a.at[1, k], near(3), s))
        if low:
            start(y == 0, lambda s: send(pa(2, k), pa(1, k), sem_a.at[1, k], near(1), s))

    def forward_second(k):
        low = k < pieces // 2

        @pl.when(y == 1)
        def _():
            arrived(pa(2, k), sem_a.at[2, k])

        @pl.when(y == 3)
        def _():
            arrived(pa(0, k), sem_a.at[0, k])

        if low:
            start(y == 1, lambda s: send(pa(2, k), pa(1, k), sem_a.at[1, k], near(2), s))
        else:
            start(y == 3, lambda s: send(pa(0, k), pa(1, k), sem_a.at[1, k], near(2), s))

    def forward_b(k, here, back):
        @pl.when(here)
        def _():
            arrived(pb(1, k), sem_b.at[1, k])

        start(here & (core == 0), lambda s: send(pb(1, k), pb(0, k), sem_b.at[0, k], (i + 1, j), s))
        if back is not None:
            start(back, lambda s: send(pb(1, k), pb(2, k), sem_b.at[2, k], (i - 1, j), s))

    lanes_first(0)
    for k in range(pieces):
        forward_first(k)
        forward_b(k, x < 3, (x < 3) & (lane > 0))
        if k > 0:
            forward_second(k - 1)
        if 0 < k < 3:
            lanes_second(k - 1)
        if k < 2:
            lanes_first(k + 1)
            start_far(k + 2)
    lanes_last(0)
    lanes_second(2)
    forward_second(pieces - 1)

    for t in range(TICKS - 1):
        arrived(ra_meta.at[t], sem_m.at[t])
        arrived(rb_meta.at[t], sem_m.at[t + 3])
    moves = [pltpu.make_async_copy(ra_meta.at[t], slot_of.at[1 + t], meta_sems.at[1 + t]) for t in range(TICKS - 1)]
    moves += [pltpu.make_async_copy(rb_meta.at[t], slot_of.at[4 + t], meta_sems.at[4 + t]) for t in range(TICKS - 1)]
    for move in moves:
        move.start()
    for move in moves:
        move.wait()

    def later_tick(t):
        if t != 2:
            for k in range(pieces):
                arrived(pb(t - 1, k), sem_b.at[t - 1, k])
        add_tick(t, 3 + t, (i + t) // n_row, rb[t - 1])

    for k in range(pieces):
        pl.when(y == 0)(lambda k=k: arrived(pa(0, k), sem_a.at[0, k]))
    expand_left(1, ra[0])
    pl.when(lane < LANES - 1)(lambda: later_tick(1))
    lanes_last(1)
    for k in range(pieces):
        arrived(pa(1, k), sem_a.at[1, k])
    expand_left(2, ra[1])
    pl.when(x < 3)(lambda: later_tick(2))
    for k in range(pieces):
        forward_b(k, lane == LANES - 2, None)
    lanes_last(2)
    for k in range(pieces):
        forward_b(k, lane == LANES - 1, lane == LANES - 1)
    for k in range(pieces):
        pl.when(y == 3)(lambda k=k: arrived(pa(2, k), sem_a.at[2, k]))
    expand_left(3, ra[2])
    pl.when(lane == LANES - 1)(lambda: later_tick(1))
    pl.when(x == 3)(lambda: later_tick(2))
    later_tick(3)
    for cond, make in pending:
        if cond is None:
            make().wait_send()
        else:
            pl.when(cond)(lambda make=make: make().wait_send())


def shards(n_row, n_col, a_blocks, a_ids, a_count, b_blocks, b_ids, b_count):
    slots = a_blocks.shape[0]
    width = a_blocks.shape[1]
    share = slots // LANES
    kind = a_blocks.dtype
    panel = (slots, width, width)
    hbm = pl.BlockSpec(memory_space=pl.ANY)
    dma = pltpu.SemaphoreType.DMA
    return pl.pallas_call(
        functools.partial(kernel, n_row, n_col),
        out_shape=jax.ShapeDtypeStruct((BR * width, BC * width), kind),
        in_specs=[hbm] * 6,
        out_specs=pl.BlockSpec(memory_space=pltpu.VMEM),
        scratch_shapes=[
            pltpu.VMEM(panel, kind) for _ in range(2 + TICKS + TICKS - 1)
        ]
        + [
            pltpu.VMEM((8, 128), jnp.int32),
            pltpu.VMEM((TICKS - 1, 8, 128), jnp.int32),
            pltpu.VMEM((TICKS - 1, 8, 128), jnp.int32),
        ]
        + [pltpu.VMEM((3, share, width, width), kind)] * 3
        + [
            pltpu.VMEM((BR * width, BK * width), kind) for _ in range(TICKS)
        ]
        + [
            pltpu.VMEM((BK * width, BC * width), kind),
            pltpu.VMEM((BR * width, BC * width), jnp.float32),
            pltpu.SMEM(a_ids.shape, jnp.int32),
            pltpu.SMEM(a_count.shape, jnp.int32),
            pltpu.SMEM(b_ids.shape, jnp.int32),
            pltpu.SMEM(b_count.shape, jnp.int32),
            pltpu.SMEM((2 * TICKS - 1, 8, 128), jnp.int32),
            dma((4, 4)), dma((3, 4)), dma((6,)), dma((3, 3)), dma((6,)), dma((7,)), dma((112,)),
        ],
        compiler_params=pltpu.CompilerParams(
            collective_id=0, has_side_effects=True, vmem_limit_bytes=60 * 1024 * 1024
        ),
        cost_estimate=pl.CostEstimate(
            flops=2 * BR * width * BC * width * TICKS * BK * width, bytes_accessed=5 * 1024 * 1024, transcendentals=0
        ),
    )(a_blocks, a_ids, a_count, b_blocks, b_ids, b_count)


def solution(mesh):
    return jax.shard_map(
        functools.partial(shards, mesh.shape["row"], mesh.shape["col"]),
        mesh=mesh,
        in_specs=(
            P("row", "col", None),
            P("row", "col"),
            P("row", "col"),
            P("row", "col", None),
            P("row", "col"),
            P("row", "col"),
        ),
        out_specs=P("row", "col"),
        check_vma=False,
    )
```

```python
import functools

import jax
import jax.numpy as jnp
from jax import lax
from jax.experimental import pallas as pl
from jax.experimental.pallas import tpu as pltpu
from jax.sharding import PartitionSpec as P

BR = 8
BK = 4
BC = 8
TICKS = 4
LANES = 8
MESH = pl.DeviceIdType.MESH


def fill(dense, blocks, place, rows, cols):
    width = blocks.shape[-1]
    for number in range(rows * cols):
        r, c = number // cols, number % cols
        slot = place(number)
        block = blocks[jnp.maximum(slot - 1, 0)]
        block = jnp.where(slot > 0, block, jnp.zeros_like(block))
        dense[r * width : (r + 1) * width, c * width : (c + 1) * width] = block


def kernel(
    n_row, n_col, a, a_ids, a_count, b, b_ids, b_count, out,
    own_a, own_b, ra0, ra1, ra2, ra3, rb0, rb1, rb2, meta, ra_meta, rb_meta, lane_in, lane_mid, lane_out, left0, left1, left2, left3, right, total,
    ids_a, count_a, ids_b, count_b, slot_of,
    sem_a, sem_b, sem_m, sem_l, local_sems, meta_sems, send_sems,
):
    ra, rb = (ra0, ra1, ra2, ra3), (rb0, rb1, rb2)
    i, j = lax.axis_index("row"), lax.axis_index("col")
    n_zlo = n_col // 4
    n_z = n_row // LANES * n_zlo
    hop = n_z // 4
    zh, lane = i // LANES, i % LANES
    x, core = lane // 2, lane % 2
    zl, y = j // 4, j % 4
    z = zh * n_zlo + zl
    slots = a.shape[0]
    width = a.shape[-1]
    pieces = 4
    part = slots // pieces
    share = slots // LANES

    locals_ = [
        pltpu.make_async_copy(a_ids, ids_a, local_sems.at[0]),
        pltpu.make_async_copy(a_count, count_a, local_sems.at[1]),
        pltpu.make_async_copy(b_ids, ids_b, local_sems.at[2]),
        pltpu.make_async_copy(b_count, count_b, local_sems.at[3]),
        pltpu.make_async_copy(a, own_a, local_sems.at[4]),
        pltpu.make_async_copy(b.at[pl.ds(0, slots)], own_b, local_sems.at[5]),
    ]
    for copy in locals_:
        copy.start()

    def along_z(steps):
        there = (z + steps + n_z) % n_z
        return ((there // n_zlo) * LANES + lane, (there % n_zlo) * 4 + y)

    barrier = pltpu.get_barrier_semaphore()
    away = hop * (1 - 2 * core)
    senders = [(zh * LANES + (lane + d) % LANES, j) for d in range(1, LANES)]
    senders += [((i + t) % n_row, j) for t in range(1, TICKS)]
    senders += [(i, (j + t) % n_col) for t in range(1, TICKS + 1)]
    senders += [(i, zl * 4 + (y + 1) % 4), (i, zl * 4 + (y + 3) % 4)]
    senders += [along_z(-away)]
    for sender in senders:
        pl.semaphore_signal(barrier, inc=1, device_id=sender, device_id_type=MESH)
    for copy in locals_[:4]:
        copy.wait()
    at_row = lax.broadcasted_iota(jnp.int32, meta.shape, 0)
    at_lane = lax.broadcasted_iota(jnp.int32, meta.shape, 1)
    found = jnp.zeros(meta.shape, jnp.int32)
    for s in range(slots):
        name = jnp.where(s < count_a[0, 0], ids_a[0, s], -1)
        found = jnp.where((at_row == 0) & (at_lane == name), s + 1, found)
        for h in range(2):
            name = jnp.where(s < count_b[0, h], ids_b[0, h * slots + s], -1)
            found = jnp.where((at_row == 1 + h) & (at_lane == name), s + 1, found)
    meta[...] = found
    mine_at = pltpu.make_async_copy(meta, slot_of.at[0], meta_sems.at[0])
    mine_at.start()
    pl.semaphore_wait(barrier, len(senders))

    pending = []

    def send(src, dst, sem, device, slot):
        return pltpu.make_async_remote_copy(
            src_ref=src, dst_ref=dst, send_sem=send_sems.at[slot], recv_sem=sem,
            device_id=device, device_id_type=MESH,
        )

    def start(cond, make):
        slot = len(pending)
        pending.append((cond, functools.partial(make, slot)))
        if cond is None:
            make(slot).start()
        else:
            pl.when(cond)(lambda: make(slot).start())

    def arrived(ref, sem):
        pltpu.make_async_copy(ref, ref, sem).wait()

    def pa(slot, k):
        return ra[slot].at[pl.ds(k * part, part)]

    def pb(slot, k):
        return rb[slot].at[pl.ds(k * part, part)]

    base = slots * (1 - zh)

    @pl.when(lane < 3)
    def _():
        pltpu.make_async_copy(
            b.at[pl.ds(base + share * lane, share)], lane_in.at[lane], sem_l.at[0, lane]
        ).start()

    for d in range(1, LANES):
        to = (lane + d) % LANES
        start(
            lane < 3,
            lambda s, to=to: send(
                b.at[pl.ds(base + share * to, share)], lane_in.at[lane], sem_l.at[0, lane], (zh * LANES + to, j), s
            ),
        )

    up = (y + 2) // 3
    far = (i, (zl - 1 + y // 3 + n_zlo) % n_zlo * 4 + (y + up) % 4)

    def start_far(k):
        mine = a.at[pl.ds(k * part, part)]
        start(y == 0, lambda s: send(mine, pa(3, k), sem_a.at[3, k], far, s))
        start(y > 0, lambda s: send(mine, pa(2, k), sem_a.at[2, k], far, s))

    for k in range(pieces):
        start_far(k)
        mine = a.at[pl.ds(k * part, part)]
        start(y > 0, lambda s, k=k, mine=mine: send(mine, pa(0, k), sem_a.at[0, k], (i, j - 1), s))
        own = b.at[pl.ds(k * part, part)]
        start(x > 0, lambda s, k=k, own=own: send(own, pb(1, k), sem_b.at[1, k], (i - 2, j), s))
        start(core == 1, lambda s, k=k, own=own: send(own, pb(0, k), sem_b.at[0, k], (i - 1, j), s))

    for t in range(1, TICKS):
        start(None, lambda s, t=t: send(meta, ra_meta.at[t - 1], sem_m.at[t - 1], (i, (j - t + n_col) % n_col), s))
        start(None, lambda s, t=t: send(meta, rb_meta.at[t - 1], sem_m.at[t + 2], ((i - t + n_row) % n_row, j), s))
    mine_at.wait()
    for copy in locals_[4:]:
        copy.wait()

    tile = 2 * width

    lefts = (left0, left1, left2, left3)

    def expand_left(t, a_panel):
        fill(lefts[t], a_panel, lambda n: slot_of[t, 0, n], BR, BK)

    def add_tick(t, b_at, half, b_panel):
        left = lefts[t]
        fill(right, b_panel, lambda n: slot_of[b_at, 1 + half, n], BK, BC)

        @pl.loop(0, BR * width // tile)
        def _(step):
            rows = pl.ds(pl.multiple_of(step * tile, tile), tile)
            product = jnp.dot(left[rows, :], right[...], preferred_element_type=jnp.float32)
            if t > 0:
                product = total[rows, :] + product
            if t < TICKS - 1:
                total[rows, :] = product
            else:
                out[rows, :] = product.astype(out.dtype)

    expand_left(0, own_a)
    add_tick(0, 0, 0, own_b)

    def lanes_first(p):
        arrived(lane_in.at[p], sem_l.at[0, p])
        start(None, lambda s: send(lane_in.at[p], lane_mid.at[p], sem_l.at[1, p], along_z(away), s))

    def lanes_second(p):
        arrived(lane_mid.at[p], sem_l.at[1, p])
        start(None, lambda s: send(lane_mid.at[p], lane_out.at[p], sem_l.at[2, p], along_z(away), s))

    def lanes_last(p):
        arrived(lane_out.at[p], sem_l.at[2, p])
        for goal, slot in (((6, 1), (5, 2)), ((7, 1),), ((7, 2),))[p]:
            into = rb[slot].at[pl.ds(lane * share, share)]
            sem = sem_b.at[slot, lane // 2]

            @pl.when(lane == goal)
            def _():
                pltpu.make_async_copy(lane_out.at[p], into, sem).start()

            start(
                lane != goal,
                lambda s, goal=goal, into=into, sem=sem: send(lane_out.at[p], into, sem, (zh * LANES + goal, j), s),
            )

    def near(to):
        return (i, zl * 4 + to)

    def forward_first(k):
        low = k < pieces // 2

        @pl.when(y == 0)
        def _():
            arrived(pa(3, k), sem_a.at[3, k])

        start(y == 0, lambda s: send(pa(3, k), pa(2, k), sem_a.at[2, k], near(1), s))
        start(y == 0, lambda s: send(pa(3, k), pa(0, k), sem_a.at[0, k], near(3), s))

        @pl.when((y == 1) | (y == 2))
        def _():
            arrived(pa(0, k), sem_a.at[0, k])

        start(y == 1, lambda s: send(pa(0, k), pa(1, k), sem_a.at[1, k], near(0), s))
        if not low:
            start(y == 2, lambda s: send(pa(0, k), pa(1, k), sem_a.at[1, k], near(1), s))

        @pl.when((y == 0) | (y == 2))
        def _():
            arrived(pa(2, k), sem_a.at[2, k])

        start(y == 2, lambda s: send(pa(2, k), pa(1, k), sem_a.at[1, k], near(3), s))
        if low:
            start(y == 0, lambda s: send(pa(2, k), pa(1, k), sem_a.at[1, k], near(1), s))

    def forward_second(k):
        low = k < pieces // 2

        @pl.when(y == 1)
        def _():
            arrived(pa(2, k), sem_a.at[2, k])

        @pl.when(y == 3)
        def _():
            arrived(pa(0, k), sem_a.at[0, k])

        if low:
            start(y == 1, lambda s: send(pa(2, k), pa(1, k), sem_a.at[1, k], near(2), s))
        else:
            start(y == 3, lambda s: send(pa(0, k), pa(1, k), sem_a.at[1, k], near(2), s))

    def forward_b(k, here, back):
        @pl.when(here)
        def _():
            arrived(pb(1, k), sem_b.at[1, k])

        start(here & (core == 0), lambda s: send(pb(1, k), pb(0, k), sem_b.at[0, k], (i + 1, j), s))
        if back is not None:
            start(back, lambda s: send(pb(1, k), pb(2, k), sem_b.at[2, k], (i - 1, j), s))

    lanes_first(0)
    for k in range(pieces):
        forward_first(k)
        forward_b(k, x < 3, (x < 3) & (lane > 0))
        if k > 0:
            forward_second(k - 1)
        if 0 < k < 3:
            lanes_second(k - 1)
        if k < 2:
            lanes_first(k + 1)
    lanes_second(2)
    lanes_last(0)
    forward_second(pieces - 1)

    for t in range(TICKS - 1):
        arrived(ra_meta.at[t], sem_m.at[t])
        arrived(rb_meta.at[t], sem_m.at[t + 3])
    moves = [pltpu.make_async_copy(ra_meta.at[t], slot_of.at[1 + t], meta_sems.at[1 + t]) for t in range(TICKS - 1)]
    moves += [pltpu.make_async_copy(rb_meta.at[t], slot_of.at[4 + t], meta_sems.at[4 + t]) for t in range(TICKS - 1)]
    for move in moves:
        move.start()
    for move in moves:
        move.wait()

    def later_tick(t):
        if t != 2:
            for k in range(pieces):
                arrived(pb(t - 1, k), sem_b.at[t - 1, k])
        add_tick(t, 3 + t, (i + t) // n_row, rb[t - 1])

    for k in range(pieces):
        pl.when(y == 0)(lambda k=k: arrived(pa(0, k), sem_a.at[0, k]))
    expand_left(1, ra[0])
    pl.when(lane < LANES - 1)(lambda: later_tick(1))
    lanes_last(1)
    for k in range(pieces):
        arrived(pa(1, k), sem_a.at[1, k])
    expand_left(2, ra[1])
    pl.when(x < 3)(lambda: later_tick(2))
    for k in range(pieces):
        forward_b(k, lane == LANES - 2, None)
    lanes_last(2)
    for k in range(pieces):
        forward_b(k, lane == LANES - 1, lane == LANES - 1)
    for k in range(pieces):
        pl.when(y == 3)(lambda k=k: arrived(pa(2, k), sem_a.at[2, k]))
    expand_left(3, ra[2])
    pl.when(lane == LANES - 1)(lambda: later_tick(1))
    pl.when(x == 3)(lambda: later_tick(2))
    later_tick(3)
    for cond, make in pending:
        if cond is None:
            make().wait_send()
        else:
            pl.when(cond)(lambda make=make: make().wait_send())


def shards(n_row, n_col, a_blocks, a_ids, a_count, b_blocks, b_ids, b_count):
    slots = a_blocks.shape[0]
    width = a_blocks.shape[1]
    share = slots // LANES
    kind = a_blocks.dtype
    panel = (slots, width, width)
    hbm = pl.BlockSpec(memory_space=pl.ANY)
    dma = pltpu.SemaphoreType.DMA
    return pl.pallas_call(
        functools.partial(kernel, n_row, n_col),
        out_shape=jax.ShapeDtypeStruct((BR * width, BC * width), kind),
        in_specs=[hbm] * 6,
        out_specs=pl.BlockSpec(memory_space=pltpu.VMEM),
        scratch_shapes=[
            pltpu.VMEM(panel, kind) for _ in range(2 + TICKS + TICKS - 1)
        ]
        + [
            pltpu.VMEM((8, 128), jnp.int32),
            pltpu.VMEM((TICKS - 1, 8, 128), jnp.int32),
            pltpu.VMEM((TICKS - 1, 8, 128), jnp.int32),
        ]
        + [pltpu.VMEM((3, share, width, width), kind)] * 3
        + [
            pltpu.VMEM((BR * width, BK * width), kind) for _ in range(TICKS)
        ]
        + [
            pltpu.VMEM((BK * width, BC * width), kind),
            pltpu.VMEM((BR * width, BC * width), jnp.float32),
            pltpu.SMEM(a_ids.shape, jnp.int32),
            pltpu.SMEM(a_count.shape, jnp.int32),
            pltpu.SMEM(b_ids.shape, jnp.int32),
            pltpu.SMEM(b_count.shape, jnp.int32),
            pltpu.SMEM((2 * TICKS - 1, 8, 128), jnp.int32),
            dma((4, 4)), dma((3, 4)), dma((6,)), dma((3, 3)), dma((6,)), dma((7,)), dma((112,)),
        ],
        compiler_params=pltpu.CompilerParams(
            collective_id=0, has_side_effects=True, vmem_limit_bytes=60 * 1024 * 1024
        ),
        cost_estimate=pl.CostEstimate(
            flops=2 * BR * width * BC * width * TICKS * BK * width, bytes_accessed=5 * 1024 * 1024, transcendentals=0
        ),
    )(a_blocks, a_ids, a_count, b_blocks, b_ids, b_count)


def solution(mesh):
    return jax.shard_map(
        functools.partial(shards, mesh.shape["row"], mesh.shape["col"]),
        mesh=mesh,
        in_specs=(
            P("row", "col", None),
            P("row", "col"),
            P("row", "col"),
            P("row", "col", None),
            P("row", "col"),
            P("row", "col"),
        ),
        out_specs=P("row", "col"),
        check_vma=False,
    )
```
